32 devices in a mesh: space: 8 (over z, x), tm: 4 (over y, core).
Axes of the slice: x: 2, y: 2, z: 4, core: 2. Of those that a mesh axis runs over, the one named last changes fastest.
Arguments:
- latent: float32 [24, 1024, 2048], P(None, 'space', 'tm'), may hold values from -1.8 to 1.8
- events: int32 [24, 1024, 2048], P(None, 'space', 'tm'), may hold values from 0 to 7
- log_base: float32 [24, 1024, 2048], P(None, 'space', 'tm'), may hold values from -1.5 to 0.5
- innovation: float32 [24, 1024, 2048], P(None, 'space', 'tm'), may hold values from -6 to 6
- kappa_sq: float32 [24, 1024], replicated, may hold values from 0.3 to 3
- chol_factor: float32 [2048, 2048], P(None, 'tm'), as said below
- step_size: float32 [1], replicated, may hold values from 0.02 to 0.08
Outputs:
- gradient: float32 [24, 1024, 2048], P(None, 'space', 'tm')
- proposal: float32 [24, 1024, 2048], P(None, 'space', 'tm')
The draws below stay inside these ranges and needn't reach their ends.
Inputs may be any that keep to these rules, and one draw needn't show every extreme that they name: chol_factor is lower triangular with a positive diagonal.
All inputs are finite; a program needn't handle non-finite values.
Results may differ from the reference program's by a relative error of at most 0.000067.
Values sent between devices are 32-bit elements; how exact they have to be, the bound alone decides.
No kernel may reach another device: no remote copies, remote signals or barrier semaphores. Data moves between devices by JAX's collectives and lax.ppermute only.
A program may use at most 128 MiB of HBM per device.

```python
import math
import jax
import jax.numpy as jnp
from jax import lax

R = 24
C = 1024
TT = 2048


def draw_chol_factor(key, part):
    key_diag, key_lower = jax.random.split(key)
    diagonal = jax.random.uniform(key_diag, (TT,), jnp.float32, 0.2, 0.45)
    lower_part = jax.random.normal(key_lower, (TT, TT), jnp.float32) * (0.4 / math.sqrt(TT))
    position = jnp.arange(TT)
    below = jnp.where(position[:, None] > position[None, :], lower_part, 0.0)
    return jnp.where(position[:, None] == position[None, :], diagonal[:, None], below)


def set_ends(result, own_key, smallest, largest):
    extent = result.shape
    place = [jax.random.randint(jax.random.fold_in(own_key, axis), (), 0, extent[axis]) for axis in range(len(extent))]
    result = result.at[tuple(place)].set(smallest)
    longest = extent.index(max(extent))
    place[longest] = (place[longest] + 1) % extent[longest]
    return result.at[tuple(place)].set(largest)


def block_scale(own_key, dims, cuts, low, high):
    gain = 1.0
    for dim, parts in cuts:
        steps = jax.random.uniform(jax.random.fold_in(jax.random.fold_in(own_key, 6), dim), (parts,), jnp.float32, low / len(cuts), high / len(cuts))
        gain = gain * jnp.repeat(jnp.exp(steps), dims[dim] // parts).reshape((-1,) + (1,) * (len(dims) - 1 - dim))
    return gain


def gaussian(key, extent, deviation, bound, shards=(), dtype=jnp.bfloat16):
    result = deviation * jax.random.normal(key, extent, jnp.float32)
    if shards:
        result = result * block_scale(key, extent, shards, -0.22, 0.18)
    return jnp.clip(result, -bound, bound).astype(dtype)


def setup_inputs(seed: int = 0) -> dict:
    streams_of = jax.random.split(jax.random.key(seed), 8)
    return {
        "latent": gaussian(streams_of[0], (R, C, TT), 0.3, 1.8, ((1, 8), (2, 4)), jnp.float32),
        "events": set_ends(jax.random.randint(streams_of[1], (R, C, TT), 0, 8), jax.random.fold_in(streams_of[1], 1), 0, 7).astype(jnp.int32),
        "log_base": jnp.clip(-1.5 + 2.0 * jax.random.uniform(streams_of[2], (R, C, TT), jnp.float32) ** block_scale(streams_of[2], (R, C, TT), ((1, 8), (2, 4)), -0.2, 0.2), -1.5, 0.5),
        "innovation": gaussian(streams_of[3], (R, C, TT), 1.0, 6.0, ((1, 8), (2, 4)), jnp.float32),
        "kappa_sq": jnp.clip(jnp.exp(jax.random.uniform(streams_of[4], (R, C), jnp.float32, math.log(0.3), math.log(3.0))), 0.3, 3.0),
        "chol_factor": draw_chol_factor(jax.random.fold_in(streams_of[7], 71), 0),
        "step_size": jnp.clip(jnp.exp(jax.random.uniform(streams_of[6], (1,), jnp.float32, math.log(0.02), math.log(0.08))), 0.02, 0.08),
    }


def operate(field, kappa_sq):
    padded = jnp.pad(field, ((1, 1), (1, 1), (0, 0)))
    beside = padded[2:, 1:-1] + padded[:-2, 1:-1]
    beside = beside + padded[1:-1, 2:] + padded[1:-1, :-2]
    return (kappa_sq[:, :, None] + 4.0) * field - beside

def reference(latent, events, log_base, innovation, kappa_sq, chol_factor, step_size):
    spatial = operate(operate(latent, kappa_sq), kappa_sq)
    flattened = spatial.reshape(R * C, TT)
    projected = jnp.dot(flattened, chol_factor, precision=lax.Precision.HIGHEST, preferred_element_type=jnp.float32)
    prior_term = jnp.dot(projected, chol_factor.T, precision=lax.Precision.HIGHEST, preferred_element_type=jnp.float32)
    prior_term = prior_term.reshape(R, C, TT)
    gradient = events.astype(jnp.float32) - jnp.exp(log_base + latent) - prior_term
    proposal = latent + step_size[0] * gradient + jnp.sqrt(2.0 * step_size[0]) * innovation
    return (gradient, proposal)
```

```python
import jax
import jax.numpy as jnp
from jax import lax
from jax.sharding import PartitionSpec as P

WIDTH = 16


def column_plan(cols):
    width = min(WIDTH, cols)
    starts = list(range(0, cols, width))
    inner = starts[1:-1]
    edges = starts[:1] + starts[-1:] if len(starts) > 1 else starts
    return [(s, width) for s in inner + edges]


def halo(latent, width):
    count = lax.axis_size("space")
    cols = latent.shape[1]
    forward = [(i, i + 1) for i in range(count - 1)]
    backward = [(i + 1, i) for i in range(count - 1)]
    low = lax.ppermute(latent[:, cols - width :], "space", forward)
    high = lax.ppermute(latent[:, :width], "space", backward)
    return low, high


def operate(extended, kappa_cols):
    centre = extended[:, 1:-1]
    row_padded = jnp.pad(centre, ((1, 1), (0, 0), (0, 0)))
    beside = row_padded[2:] + row_padded[:-2]
    beside = beside + extended[:, 2:] + extended[:, :-2]
    return (kappa_cols[:, :, None] + 4.0) * centre - beside


def local(latent, events, log_base, innovation, kappa_sq, chol_factor, step_size):
    rows, cols, hours = latent.shape
    size = lax.axis_size("tm")
    group = size // 2
    place = lax.axis_index("tm")
    half = place // group
    core = place % group
    part = rows // group
    space_index = lax.axis_index("space")
    space_count = lax.axis_size("space")

    def index(upper, member):
        return upper * group + member % group

    def within(x, shift):
        pairs = [(index(u, m), index(u, m + shift)) for u in (0, 1) for m in range(group)]
        return lax.ppermute(x, "tm", pairs)

    def up(x):
        return lax.ppermute(x, "tm", [(index(1, m), index(0, m)) for m in range(group)])

    def down(x):
        return lax.ppermute(x, "tm", [(index(0, m), index(1, m)) for m in range(group)])

    def block(x, member):
        return lax.dynamic_slice_in_dim(x, member % group * part, part, axis=0)

    columns = jnp.concatenate([chol_factor] + [within(chol_factor, j) for j in range(1, group)], axis=1)

    def factor_block(upper, shift):
        return lax.dynamic_slice_in_dim(columns, (upper * group + (core - shift) % group) * hours, hours, axis=0)

    factor = jnp.concatenate(
        [factor_block(half, j) for j in range(group)] + [factor_block(1 - half, j) for j in range(group)], axis=0
    )

    low, high = halo(latent, 2)
    padded_kappa = jnp.pad(kappa_sq, ((0, 0), (1, 1)))
    kappa_wide = lax.dynamic_slice(padded_kappa, (jnp.int32(0), space_index * cols), (rows, cols + 2))

    def filtered(start, width):
        left, right = start - 2, start + width + 2
        pieces = []
        if left < 0:
            pieces.append(low)
        pieces.append(latent[:, max(left, 0) : min(right, cols)])
        if right > cols:
            pieces.append(high)
        wide = jnp.concatenate(pieces, axis=1) if len(pieces) > 1 else pieces[0]
        once = operate(wide, kappa_wide[:, start : start + width + 2])
        position = space_index * cols + start - 1 + jnp.arange(width + 2)
        inside = (position >= 0) & (position < space_count * cols)
        once = jnp.where(inside[None, :, None], once, 0.0)
        return operate(once, kappa_wide[:, start + 1 : start + width + 1])

    step = step_size[0]
    spread = jnp.sqrt(2.0 * step)
    gradient = jnp.zeros(latent.shape, jnp.float32)
    proposal = jnp.zeros(latent.shape, jnp.float32)
    for start, width in column_plan(cols):
        spatial = filtered(start, width)
        arrived = up(spatial)
        own = [block(spatial, core)] + [within(block(spatial, core + j), j) for j in range(1, group)]
        other = [block(arrived, core)] + [within(block(arrived, core + j), j) for j in range(1, group)]
        cells = part * width
        series = jnp.concatenate([x.reshape(cells, hours) for x in own + other], axis=1)
        projected = jnp.dot(series, factor, precision=lax.Precision.HIGH, preferred_element_type=jnp.float32)
        summed = lax.dot_general(
            projected,
            factor,
            (((1,), (1,)), ((), ())),
            precision=lax.Precision.HIGH,
            preferred_element_type=jnp.float32,
        )
        total = summed[:, : group * hours] + down(summed[:, group * hours :])
        prior = jnp.zeros((rows, width, hours), jnp.float32)
        for j in range(group):
            piece = total[:, j * hours : (j + 1) * hours]
            piece = (within(piece, -j) if j else piece).reshape(part, width, hours)
            prior = lax.dynamic_update_slice_in_dim(prior, piece, (core + j) % group * part, axis=0)
        here = slice(start, start + width)
        slope = events[:, here].astype(jnp.float32) - jnp.exp(log_base[:, here] + latent[:, here]) - prior
        gradient = gradient.at[:, here].set(slope)
        proposal = proposal.at[:, here].set(latent[:, here] + step * slope + spread * innovation[:, here])
    return gradient, proposal


def solution(mesh):
    in_specs = (
        P(None, "space", "tm"),
        P(None, "space", "tm"),
        P(None, "space", "tm"),
        P(None, "space", "tm"),
        P(),
        P(None, "tm"),
        P(),
    )
    out_specs = (P(None, "space", "tm"), P(None, "space", "tm"))
    return jax.shard_map(local, mesh=mesh, in_specs=in_specs, out_specs=out_specs, check_vma=False)
```

```python
import functools

import jax
import jax.numpy as jnp
from jax import lax
from jax.experimental import pallas as pl
from jax.experimental.pallas import tpu as pltpu
from jax.sharding import PartitionSpec as P

EDGE = 8
LANES = 128
WIDTH = 32
FACTOR_BLOCK = 256
VMEM_LIMIT = 54 * 1024 * 1024
EARLY_LIMIT = 60 * 1024 * 1024
PRODUCT_LIMIT = 50 * 1024 * 1024
LIGHT = pl.CostEstimate(flops=0, bytes_accessed=4096, transcendentals=0)


def split_bf16(x):
    high = x.astype(jnp.bfloat16)
    return high, (x - high.astype(jnp.float32)).astype(jnp.bfloat16)


def anywhere(count):
    return [pl.BlockSpec(memory_space=pl.ANY)] * count


def in_vmem(count):
    return [pl.BlockSpec(memory_space=pltpu.VMEM)] * count


def start(group):
    for copy in group:
        copy.start()


def wait(group):
    for copy in group:
        copy.wait()


def split_rows(where_ref, own, beside, first, held, sems, targets):
    size, width = targets[0].shape[0], own.shape[1]
    step = held.shape[2]
    places = (where_ref[1], 1 - where_ref[1])
    groups = [
        [
            pltpu.make_async_copy(source.at[pl.ds(first + row, step)], held.at[i, j], sems.at[i, j])
            for j, source in enumerate((own, beside))
        ]
        for i, row in enumerate(range(0, size, step))
    ]
    for copies in groups:
        start(copies)
    for i, copies in enumerate(groups):
        wait(copies)
        for j, place in enumerate(places):
            at = pl.ds(pl.multiple_of(place * width, width), width)
            for ref, value in zip(targets, split_bf16(held[i, j])):
                ref[i * step : (i + 1) * step, at] = value


def diagonal_kernel(tokens, where_ref, own, beside, *refs):
    *targets, held, sems = refs[tokens:]
    split_rows(where_ref, own, beside, where_ref[0] * targets[0].shape[0], held, sems, targets)


def split_scratch(size, width):
    step = min(FACTOR_BLOCK, size)
    return [pltpu.VMEM((size // step, 2, step, width), jnp.float32), pltpu.SemaphoreType.DMA((size // step, 2))]


def split_diagonal(where, own, beside, after):
    hours, width = own.shape
    half = hours // 2
    return pl.pallas_call(
        functools.partial(diagonal_kernel, len(after)),
        in_specs=[pl.BlockSpec(memory_space=pltpu.SMEM)] + anywhere(2 + len(after)),
        out_specs=in_vmem(2),
        out_shape=[jax.ShapeDtypeStruct((half, 2 * width), jnp.bfloat16)] * 2,
        scratch_shapes=split_scratch(half, width),
        compiler_params=pltpu.CompilerParams(vmem_limit_bytes=PRODUCT_LIMIT),
        cost_estimate=LIGHT,
        name="split_diagonal",
    )(where, own, beside, *after)


def below_kernel(tokens, where_ref, order_ref, own, beside, *refs):
    gathered, refs = refs[:4], refs[4 + tokens :]
    *targets, held, sems, parts, part_sems = refs
    size, width = targets[0].shape[0], own.shape[1]

    @pl.when(where_ref[0] == 0)
    def _():
        split_rows(where_ref, own, beside, size, held, sems, targets)

    @pl.when(where_ref[0] != 0)
    def _():
        count, step = gathered[0].shape[:2]
        copies = [pltpu.make_async_copy(ref, parts.at[i], part_sems.at[i]) for i, ref in enumerate(gathered)]
        start(copies)
        for i, copy in enumerate(copies):
            copy.wait()
            place = where_ref[1] if i < 2 else 1 - where_ref[1]
            at = pl.ds(pl.multiple_of(place * width, width), width)
            for j in range(count):
                rows = pl.ds(pl.multiple_of(order_ref[i % 2 * count + j] * step, step), step)
                for ref, value in zip(targets, split_bf16(parts[i, j])):
                    ref[rows, at] = value


def split_below(where, order, own, beside, gathered, after):
    hours, width = own.shape
    half = hours // 2
    return pl.pallas_call(
        functools.partial(below_kernel, len(after)),
        in_specs=[pl.BlockSpec(memory_space=pltpu.SMEM)] * 2 + anywhere(6 + len(after)),
        out_specs=in_vmem(2),
        out_shape=[jax.ShapeDtypeStruct((half, 2 * width), jnp.bfloat16)] * 2,
        scratch_shapes=split_scratch(half, width)
        + [pltpu.VMEM((4, *gathered[0].shape), jnp.float32), pltpu.SemaphoreType.DMA((4,))],
        compiler_params=pltpu.CompilerParams(vmem_limit_bytes=PRODUCT_LIMIT),
        cost_estimate=LIGHT,
        name="split_below",
    )(where, order, own, beside, *gathered, *after)


def filter_kernel(first_col, cols, space_count, where_ref, left, centre, right, weight_ref, *refs):
    mine_ref, other_ref, wide, once, scale = refs[-5:]
    rows, width, lanes = centre.shape
    around = width + 2 * EDGE
    core, space = where_ref[1], where_ref[2]
    zero = jnp.zeros((around, lanes), jnp.float32)
    for ref in (wide, once):
        ref[0] = zero
        ref[rows + 1] = zero
    wide[1 : rows + 1, EDGE - left.shape[1] : EDGE, :] = left[...]
    wide[1 : rows + 1, EDGE : EDGE + width, :] = centre[...]
    wide[1 : rows + 1, EDGE + width : EDGE + width + right.shape[1], :] = right[...]

    @pl.when(pl.program_id(0) == 0)
    def _():
        for row in range(rows):
            scale[row] = jnp.broadcast_to(weight_ref[first_col : first_col + around, row : row + 1], scale.shape[1:])

    strip = scale.shape[2]
    column = space * cols + first_col - EDGE + lax.broadcasted_iota(jnp.int32, (around, strip), 0)
    inside = (column >= 0) & (column < space_count * cols)

    def operate(source, row, at):
        x = source[row + 1, :, at]
        beside = source[row, :, at] + source[row + 2, :, at] + pltpu.roll(x, 1, 0) + pltpu.roll(x, around - 1, 0)
        return scale[row] * x - beside

    for place in range(lanes // strip):
        at = slice(place * strip, (place + 1) * strip)

        def first(row, carry):
            value = operate(wide, row, at)
            if first_col == 0 or first_col + width == cols:
                value = jnp.where(inside, value, 0.0)
            once[row + 1, :, at] = value
            return carry

        def second(row, carry):
            mine_ref[row, :, at] = operate(once, row + core * (rows // 2), at)[EDGE : EDGE + width]
            other_ref[row, :, at] = operate(once, row + (1 - core) * (rows // 2), at)[EDGE : EDGE + width]
            return carry

        lax.fori_loop(0, rows, first, 0, unroll=4)
        lax.fori_loop(0, rows // 2, second, 0, unroll=2)


def filtered(where, latent, halos, weights, start, width, space_count, after, limit):
    rows, cols, hours = latent.shape
    lanes = min(2 * LANES, hours)
    last = start + width

    def spec(columns, index):
        return pl.BlockSpec((rows, columns, lanes), lambda i, w: (0, index, i))

    low, high = halos
    left = (low, spec(low.shape[1], 0)) if start == 0 else (latent, spec(EDGE, start // EDGE - 1))
    centre = (latent, spec(width, start // width))
    right = (high, spec(high.shape[1], 0)) if last == cols else (latent, spec(EDGE, last // EDGE))
    fields, specs = zip(left, centre, right)
    half = rows // 2
    return pl.pallas_call(
        functools.partial(filter_kernel, start, cols, space_count),
        grid_spec=pltpu.PrefetchScalarGridSpec(
            num_scalar_prefetch=1,
            grid=(hours // lanes,),
            in_specs=[*specs, pl.BlockSpec(weights.shape, lambda i, w: (0, 0))] + anywhere(len(after)),
            out_specs=[pl.BlockSpec((half, width, lanes), lambda i, w: (0, 0, i))] * 2,
            scratch_shapes=[pltpu.VMEM((rows + 2, width + 2 * EDGE, lanes), jnp.float32)] * 2
            + [pltpu.VMEM((rows, width + 2 * EDGE, min(LANES, hours)), jnp.float32)],
        ),
        out_shape=[jax.ShapeDtypeStruct((half, width, hours), jnp.float32)] * 2,
        compiler_params=pltpu.CompilerParams(vmem_limit_bytes=limit),
        cost_estimate=LIGHT,
        name="filter",
    )(where, *fields, weights, *after)


def multiply(parts, weights, contract):
    (x_high, x_low), (w_high, w_low) = parts, weights
    dot = functools.partial(
        lax.dot_general,
        dimension_numbers=(((1,), (contract,)), ((), ())),
        preferred_element_type=jnp.float32,
    )
    return dot(x_high, w_high) + (dot(x_low, w_high) + dot(x_high, w_low))


def cut(refs, rows, columns):
    return tuple(ref[rows, columns] for ref in refs)


def blocks(size):
    step = min(FACTOR_BLOCK, size // 2)
    return [slice(i, i + step) for i in range(0, size, step)]


def place_series(source, parts):
    hours = source.shape[2]
    for place in range(2):
        for ref, value in zip(parts, split_bf16(source[place])):
            ref[:, place * hours : (place + 1) * hours] = value


def hours_of(at, size):
    place = at.start // (size // 2)
    return place, slice(at.start - place * size // 2, at.stop - place * size // 2)


def begin_kernel(tokens, where_ref, mine, across, *refs):
    refs = refs[tokens:]
    diagonal, sent, sums, fields, series, middle, held, sems = refs[:2], *refs[2:]
    size = held.shape[1]
    core = where_ref[1]
    everything = slice(None)
    series, middle = [series.at[i] for i in range(2)], [middle.at[i] for i in range(2)]
    lower = where_ref[0] == 0
    upper = jnp.logical_not(lower)
    inputs = [
        pltpu.make_async_copy(mine, fields.at[core], sems.at[0]),
        pltpu.make_async_copy(across, fields.at[1 - core], sems.at[1]),
    ]
    hours = size // 2
    forward = [
        pltpu.make_async_copy(fields.at[i], sent.at[:, i * hours : (i + 1) * hours], sems.at[2 + i]) for i in range(2)
    ]
    start(inputs)
    wait(inputs)

    @pl.when(upper)
    def _():
        start(forward)

    place_series(fields, series)
    for at in blocks(size):
        rows = slice(at.start, size)
        value = multiply(cut(series, everything, rows), cut(diagonal, rows, at), 0)

        @pl.when(lower)
        def _():
            held[:, at] = value

        @pl.when(upper)
        def _():
            for ref, part in zip(middle, split_bf16(value)):
                ref[:, at] = part

    @pl.when(lower)
    def _():
        output = pltpu.make_async_copy(held, sent, sems.at[4])
        output.start()
        output.wait()

    @pl.when(upper)
    def _():
        for at in blocks(size):
            columns = slice(0, at.stop)
            held[:, at] = multiply(cut(middle, everything, columns), cut(diagonal, at, columns), 1)
        output = pltpu.make_async_copy(held, sums, sems.at[4])
        output.start()
        wait(forward)
        output.wait()


def begin(where, mine, across, diagonal, after):
    cells, hours = mine.shape
    size = 2 * hours
    operands = [mine, across, *after]
    return pl.pallas_call(
        functools.partial(begin_kernel, len(after)),
        in_specs=[pl.BlockSpec(memory_space=pltpu.SMEM)] + anywhere(len(operands)) + in_vmem(2),
        out_specs=anywhere(2),
        out_shape=[jax.ShapeDtypeStruct((cells, size), jnp.float32)] * 2,
        scratch_shapes=[
            pltpu.VMEM((2, cells, hours), jnp.float32),
            pltpu.VMEM((2, cells, size), jnp.bfloat16),
            pltpu.VMEM((2, cells, size), jnp.bfloat16),
            pltpu.VMEM((cells, size), jnp.float32),
            pltpu.SemaphoreType.DMA((5,)),
        ],
        compiler_params=pltpu.CompilerParams(vmem_limit_bytes=PRODUCT_LIMIT),
        cost_estimate=LIGHT,
        name="begin",
    )(where, *operands, *diagonal)


def send_hours(core, place, results, targets, sem):
    for target, chosen in zip(targets, (core == place, core != place)):

        @pl.when(chosen)
        def _():
            pltpu.make_async_copy(results.at[place], target, sem).start()


def wait_hours(core, results, targets, sems):
    for place in range(2):
        for target, chosen in zip(targets, (core == place, core != place)):

            @pl.when(chosen)
            def _():
                pltpu.make_async_copy(results.at[place], target, sems[place]).wait()


def end_kernel(tokens, where_ref, sent, sums, arrived, *refs):
    refs = refs[tokens:]
    diagonal, below, targets, refs = refs[:2], refs[2:4], refs[4:6], refs[6:]
    factors, terms, held, series, middle, results, sems = refs
    size = factors.shape[1]
    core = where_ref[1]
    everything = slice(None)
    series, middle = [series.at[i] for i in range(2)], [middle.at[i] for i in range(2)]
    lower = where_ref[0] == 0
    upper = jnp.logical_not(lower)

    def inputs(field, term):
        return [
            pltpu.make_async_copy(field, factors, sems.at[0]),
            pltpu.make_async_copy(term, terms, sems.at[1]),
        ]

    before = pltpu.make_async_copy(sums, held, sems.at[2])

    @pl.when(lower)
    def _():
        start(inputs(arrived, sent))

    @pl.when(upper)
    def _():
        start(inputs(sent, arrived))
        before.start()

    @pl.when(lower)
    def _():
        wait(inputs(arrived, sent))

    @pl.when(upper)
    def _():
        wait(inputs(sent, arrived))

    for ref, part in zip(series, split_bf16(factors[...])):
        ref[...] = part
    for at in blocks(size):
        value = terms[:, at] + multiply(cut(series, everything, everything), cut(below, everything, at), 0)
        for ref, part in zip(middle, split_bf16(value)):
            ref[:, at] = part

    @pl.when(upper)
    def _():
        before.wait()

    for at in blocks(size):
        columns = slice(0, at.stop)
        place, piece = hours_of(at, size)

        @pl.when(lower)
        def _():
            results[place, :, piece] = multiply(cut(middle, everything, columns), cut(diagonal, at, columns), 1)

        @pl.when(upper)
        def _():
            value = multiply(cut(middle, everything, everything), cut(below, at, everything), 1)
            results[place, :, piece] = held[:, at] + value

        if at.stop == (place + 1) * size // 2:
            send_hours(core, place, results, targets, sems.at[3 + place])
    wait_hours(core, results, targets, [sems.at[3], sems.at[4]])


def end(where, sent, sums, arrived, diagonal, below, after):
    cells, size = sent.shape
    hours = size // 2
    operands = [sent, sums, arrived, *after]
    return pl.pallas_call(
        functools.partial(end_kernel, len(after)),
        in_specs=[pl.BlockSpec(memory_space=pltpu.SMEM)] + anywhere(len(operands)) + in_vmem(4),
        out_specs=anywhere(2),
        out_shape=[jax.ShapeDtypeStruct((cells, hours), jnp.float32)] * 2,
        scratch_shapes=[pltpu.VMEM((cells, size), jnp.float32)] * 3
        + [pltpu.VMEM((2, cells, size), jnp.bfloat16)] * 2
        + [pltpu.VMEM((2, cells, hours), jnp.float32), pltpu.SemaphoreType.DMA((5,))],
        compiler_params=pltpu.CompilerParams(vmem_limit_bytes=PRODUCT_LIMIT),
        cost_estimate=LIGHT,
        name="end",
    )(where, *operands, *diagonal, *below)


def join_kernel(count, *refs):
    out, held, sems = refs[-3:]
    first = 0
    group = []
    for i, ref in enumerate(refs[:count]):
        group.append(pltpu.make_async_copy(ref, held.at[pl.ds(first, ref.shape[0])], sems.at[i]))
        first += ref.shape[0]
    start(group)
    wait(group)
    output = pltpu.make_async_copy(held, out, sems.at[count])
    output.start()
    output.wait()


def join(pieces, after):
    shape = (sum(x.shape[0] for x in pieces), *pieces[0].shape[1:])
    return pl.pallas_call(
        functools.partial(join_kernel, len(pieces)),
        in_specs=anywhere(len(pieces) + len(after)),
        out_specs=pl.BlockSpec(memory_space=pl.ANY),
        out_shape=jax.ShapeDtypeStruct(shape, pieces[0].dtype),
        scratch_shapes=[pltpu.VMEM(shape, pieces[0].dtype), pltpu.SemaphoreType.DMA((len(pieces) + 1,))],
        compiler_params=pltpu.CompilerParams(vmem_limit_bytes=VMEM_LIMIT),
        cost_estimate=LIGHT,
        name="join",
    )(*pieces, *after)


def finish_kernel(where_ref, step_ref, own, beside, latent_ref, events_ref, base_ref, draw_ref, *refs):
    gradient_ref, proposal_ref = refs[-2:]
    latent = latent_ref[...]
    spread = jnp.sqrt(jnp.full((1, 1, latent.shape[2]), 2.0 * step_ref[0]))
    data = events_ref[...].astype(jnp.float32) - jnp.exp(base_ref[...] + latent)
    for turn, prior in enumerate((own, beside)):

        @pl.when(pl.program_id(0) == turn)
        def _():
            slope = data - prior[...]
            gradient_ref[...] = slope
            proposal_ref[...] = latent + step_ref[0] * slope + spread * draw_ref[...]


def finish(where, steps, priors, fields, start, width, outs, after):
    rows, cols, hours = fields[0].shape
    half = rows // 2
    shape = (half, width, hours)
    held = [prior.reshape(shape) for prior in priors]
    held_spec = pl.BlockSpec(shape, lambda i, w, s: (0, 0, 0))
    field_spec = pl.BlockSpec(shape, lambda i, w, s: ((w[1] + i) % 2, start // width, 0))
    out = jax.ShapeDtypeStruct((rows, cols, hours), jnp.float32)
    return pl.pallas_call(
        finish_kernel,
        grid_spec=pltpu.PrefetchScalarGridSpec(
            num_scalar_prefetch=2,
            grid=(2,),
            in_specs=[held_spec] * 2 + [field_spec] * 4 + anywhere(len(outs) + len(after)),
            out_specs=[field_spec] * 2,
        ),
        out_shape=[out, out],
        input_output_aliases={8 + i: i for i in range(len(outs))},
        compiler_params=pltpu.CompilerParams(vmem_limit_bytes=VMEM_LIMIT),
        cost_estimate=LIGHT,
        name="finish",
    )(where, steps, *held, *fields, *outs, *after)


def column_plan(cols):
    starts = list(range(0, cols, WIDTH))
    return [(s, WIDTH) for s in starts[1:-1] + [starts[0], starts[-1]]]


def local(latent, events, log_base, innovation, kappa_sq, chol_factor, step_size):
    rows, cols, hours = latent.shape
    place = lax.axis_index("tm")
    upper, core = place // 2, place % 2
    space = lax.axis_index("space")
    space_count = lax.axis_size("space")
    where = jnp.stack([upper, core, space]).astype(jnp.int32)

    def beside(x):
        return lax.ppermute(x, "tm", [(0, 1), (1, 0), (2, 3), (3, 2)])

    def exchange(x):
        return lax.ppermute(x, "tm", [(0, 2), (1, 3), (2, 0), (3, 1)])

    across_core = beside(chol_factor)
    forward = [(i, i + 1) for i in range(space_count - 1)]
    backward = [(i + 1, i) for i in range(space_count - 1)]
    halos = (
        lax.ppermute(latent[:, cols - 2 :], "space", forward),
        lax.ppermute(latent[:, :2], "space", backward),
    )
    padded = jnp.pad(kappa_sq, ((0, 0), (EDGE, EDGE))) + 4.0
    weights = lax.dynamic_slice(padded, (jnp.int32(0), space * cols), (rows, cols + 2 * EDGE)).T
    plan = column_plan(cols)
    fields = (latent, events, log_base, innovation)
    mine, others, sent, sums, arrived, totals = ({} for _ in range(6))

    def make_field(k, after, limit=VMEM_LIMIT):
        made = filtered(where, latent, halos, weights, *plan[k], space_count, after, limit)
        mine[k], away = (x.reshape(-1, hours) for x in made)
        others[k] = beside(away)

    def begin_chunk(k, after):
        sent[k], sums[k] = begin(where, mine[k], others[k], diagonal, after)
        arrived[k] = exchange(sent[k])

    def end_chunk(k, after):
        own, across = end(where, sent[k], sums[k], arrived[k], diagonal, below, after)
        totals[k] = own, beside(across)

    def finish_chunk(k, after):
        return finish(where, step_size, totals[k], fields, *plan[k], outs, after)

    share = 2 * hours // space_count
    slab = lax.dynamic_slice(chol_factor, (2 * hours + space * share, jnp.int32(0)), (share, hours))
    slab = lax.ppermute(slab, "tm", [(0, 2), (1, 3)])[None]
    order = [0]

    def double(x):
        bit = space_count // 2 // len(order)
        order.extend([i ^ bit for i in order])
        return lax.ppermute(x, "space", [(i, i ^ bit) for i in range(space_count)])

    outs = []
    make_field(0, [], EARLY_LIMIT)
    diagonal = split_diagonal(where, chol_factor, across_core, [mine[0]])
    begin_chunk(0, [])
    held = join([slab], [sent[0]])
    received = double(held)
    make_field(1, [held, *halos])
    begin_chunk(1, [])
    held = join([held, received], [sent[1]])
    received = double(held)
    make_field(2, [held])
    begin_chunk(2, [])
    held = join([held, received], [sent[2], arrived[0]])
    received = double(held)
    make_field(3, [held])
    begin_chunk(3, [])
    gathered = [held, received, beside(held), beside(received)]
    order = space.astype(jnp.int32) ^ jnp.array(order, jnp.int32)
    below = split_below(where, order, chol_factor, across_core, gathered, [sent[3], arrived[1]])
    end_chunk(0, [])
    end_chunk(1, [totals[0][0]])
    outs = finish_chunk(0, [totals[1][0]])
    end_chunk(2, [outs[0]])
    outs = finish_chunk(1, [totals[2][0]])
    outs = finish_chunk(2, [])
    end_chunk(3, [outs[0]])
    return finish_chunk(3, [])


def plain(latent, events, log_base, innovation, kappa_sq, chol_factor, step_size):
    rows, cols, hours = latent.shape
    space = lax.axis_index("space")
    count = lax.axis_size("space")
    forward = [(i, i + 1) for i in range(count - 1)]
    backward = [(i + 1, i) for i in range(count - 1)]
    kappa = lax.dynamic_slice(kappa_sq, (jnp.int32(0), space * cols), (rows, cols))

    def operate(field):
        low = lax.ppermute(field[:, -1:], "space", forward)
        high = lax.ppermute(field[:, :1], "space", backward)
        row_padded = jnp.pad(field, ((1, 1), (0, 0), (0, 0)))
        wide = jnp.concatenate([low, field, high], axis=1)
        beside = row_padded[2:] + row_padded[:-2] + wide[:, 2:] + wide[:, :-2]
        return (kappa[:, :, None] + 4.0) * field - beside

    dot = functools.partial(lax.dot_general, precision=lax.Precision.HIGHEST, preferred_element_type=jnp.float32)
    series = operate(operate(latent)).reshape(rows * cols, hours)
    projected = dot(lax.all_gather(series, "tm", axis=1, tiled=True), chol_factor, (((1,), (0,)), ((), ())))
    sums = dot(chol_factor, projected, (((1,), (1,)), ((), ())))
    by_hour = lax.psum_scatter(sums, "tm", scatter_dimension=0, tiled=True)
    prior = by_hour.T.reshape(rows, cols, hours)
    gradient = events.astype(jnp.float32) - jnp.exp(log_base + latent) - prior
    proposal = latent + step_size[0] * gradient + jnp.sqrt(2.0 * step_size[0]) * innovation
    return gradient, proposal


def solution(mesh):
    in_specs = (
        P(None, "space", "tm"),
        P(None, "space", "tm"),
        P(None, "space", "tm"),
        P(None, "space", "tm"),
        P(),
        P(None, "tm"),
        P(),
    )
    out_specs = (P(None, "space", "tm"), P(None, "space", "tm"))
    body = local if mesh.shape["tm"] == 4 and mesh.shape["space"] == 8 else plain
    return jax.shard_map(body, mesh=mesh, in_specs=in_specs, out_specs=out_specs, check_vma=False)
```

```python
import functools

import jax
import jax.numpy as jnp
from jax import lax
from jax.experimental import pallas as pl
from jax.experimental.pallas import tpu as pltpu
from jax.sharding import PartitionSpec as P

EDGE = 8
LANES = 128
WIDTH = 32
FACTOR_BLOCK = 256
VMEM_LIMIT = 60 * 1024 * 1024
LIGHT = pl.CostEstimate(flops=0, bytes_accessed=4096, transcendentals=0)


def split_bf16(x):
    high = x.astype(jnp.bfloat16)
    return high, (x - high.astype(jnp.float32)).astype(jnp.bfloat16)


def anywhere(count):
    return [pl.BlockSpec(memory_space=pl.ANY)] * count


def in_vmem(count):
    return [pl.BlockSpec(memory_space=pltpu.VMEM)] * count


def start(group):
    for copy in group:
        copy.start()


def wait(group):
    for copy in group:
        copy.wait()


def split_rows(where_ref, own, beside, first, held, sems, targets):
    size, width = targets[0].shape[0], own.shape[1]
    step = held.shape[2]
    places = (where_ref[1], 1 - where_ref[1])
    groups = [
        [
            pltpu.make_async_copy(source.at[pl.ds(first + row, step)], held.at[i, j], sems.at[i, j])
            for j, source in enumerate((own, beside))
        ]
        for i, row in enumerate(range(0, size, step))
    ]
    for copies in groups:
        start(copies)
    for i, copies in enumerate(groups):
        wait(copies)
        for j, place in enumerate(places):
            store_columns(targets, place, slice(i * step, (i + 1) * step), held[i, j])


def store_columns(targets, place, rows, values):
    width = values.shape[1]
    at = pl.ds(pl.multiple_of(place * width, width), width)
    for ref, value in zip(targets, split_bf16(values)):
        ref[rows, at] = value


def diagonal_kernel(tokens, where_ref, own, beside, *refs):
    *targets, held, sems = refs[tokens:]
    split_rows(where_ref, own, beside, where_ref[0] * targets[0].shape[0], held, sems, targets)


def split_scratch(size, width):
    step = min(FACTOR_BLOCK, size)
    return [pltpu.VMEM((size // step, 2, step, width), jnp.float32), pltpu.SemaphoreType.DMA((size // step, 2))]


def split_diagonal(where, own, beside, after):
    hours, width = own.shape
    half = hours // 2
    return pl.pallas_call(
        functools.partial(diagonal_kernel, len(after)),
        in_specs=[pl.BlockSpec(memory_space=pltpu.SMEM)] + anywhere(2 + len(after)),
        out_specs=in_vmem(2),
        out_shape=[jax.ShapeDtypeStruct((half, 2 * width), jnp.bfloat16)] * 2,
        scratch_shapes=split_scratch(half, width),
        compiler_params=pltpu.CompilerParams(vmem_limit_bytes=VMEM_LIMIT),
        cost_estimate=LIGHT,
        name="split_diagonal",
    )(where, own, beside, *after)


def below_kernel(tokens, where_ref, order_ref, own, beside, *refs):
    gathered, refs = refs[:4], refs[4 + tokens :]
    *targets, held, sems, parts, part_sems = refs
    size = targets[0].shape[0]

    @pl.when(where_ref[0] == 0)
    def _():
        split_rows(where_ref, own, beside, size, held, sems, targets)

    @pl.when(where_ref[0] != 0)
    def _():
        count, step = gathered[0].shape[:2]
        copies = [pltpu.make_async_copy(ref, parts.at[i], part_sems.at[i]) for i, ref in enumerate(gathered)]
        start(copies)
        for i, copy in enumerate(copies):
            copy.wait()
            place = where_ref[1] if i < 2 else 1 - where_ref[1]
            for j in range(count):
                rows = pl.ds(pl.multiple_of(order_ref[i % 2 * count + j] * step, step), step)
                store_columns(targets, place, rows, parts[i, j])


def split_below(where, order, own, beside, gathered, after):
    hours, width = own.shape
    half = hours // 2
    return pl.pallas_call(
        functools.partial(below_kernel, len(after)),
        in_specs=[pl.BlockSpec(memory_space=pltpu.SMEM)] * 2 + anywhere(6 + len(after)),
        out_specs=in_vmem(2),
        out_shape=[jax.ShapeDtypeStruct((half, 2 * width), jnp.bfloat16)] * 2,
        scratch_shapes=split_scratch(half, width)
        + [pltpu.VMEM((4, *gathered[0].shape), jnp.float32), pltpu.SemaphoreType.DMA((4,))],
        compiler_params=pltpu.CompilerParams(vmem_limit_bytes=VMEM_LIMIT),
        cost_estimate=LIGHT,
        name="split_below",
    )(where, order, own, beside, *gathered, *after)


def filter_kernel(first_col, cols, space_count, where_ref, left, centre, right, weight_ref, *refs):
    mine_ref, other_ref, wide, once, scale = refs[-5:]
    rows, width, lanes = centre.shape
    around = width + 2 * EDGE
    core, space = where_ref[1], where_ref[2]
    zero = jnp.zeros((around, lanes), jnp.float32)
    for ref in (wide, once):
        ref[0] = zero
        ref[rows + 1] = zero
    wide[1 : rows + 1, EDGE - left.shape[1] : EDGE, :] = left[...]
    wide[1 : rows + 1, EDGE : EDGE + width, :] = centre[...]
    wide[1 : rows + 1, EDGE + width : EDGE + width + right.shape[1], :] = right[...]

    @pl.when(pl.program_id(0) == 0)
    def _():
        for row in range(rows):
            scale[row] = jnp.broadcast_to(weight_ref[first_col : first_col + around, row : row + 1], scale.shape[1:])

    strip = scale.shape[2]
    column = space * cols + first_col - EDGE + lax.broadcasted_iota(jnp.int32, (around, strip), 0)
    inside = (column >= 0) & (column < space_count * cols)

    def operate(source, row, at):
        x = source[row + 1, :, at]
        beside = source[row, :, at] + source[row + 2, :, at] + pltpu.roll(x, 1, 0) + pltpu.roll(x, around - 1, 0)
        return scale[row] * x - beside

    for place in range(lanes // strip):
        at = slice(place * strip, (place + 1) * strip)

        def first(row, carry):
            value = operate(wide, row, at)
            if first_col == 0 or first_col + width == cols:
                value = jnp.where(inside, value, 0.0)
            once[row + 1, :, at] = value
            return carry

        def second(row, carry):
            mine_ref[row, :, at] = operate(once, row + core * (rows // 2), at)[EDGE : EDGE + width]
            other_ref[row, :, at] = operate(once, row + (1 - core) * (rows // 2), at)[EDGE : EDGE + width]
            return carry

        lax.fori_loop(0, rows, first, 0, unroll=4)
        lax.fori_loop(0, rows // 2, second, 0, unroll=2)


def filtered(where, latent, halos, weights, start, width, space_count, after):
    rows, cols, hours = latent.shape
    lanes = min(2 * LANES, hours)
    last = start + width

    def spec(columns, index):
        return pl.BlockSpec((rows, columns, lanes), lambda i, w: (0, index, i))

    low, high = halos
    left = (low, spec(low.shape[1], 0)) if start == 0 else (latent, spec(EDGE, start // EDGE - 1))
    centre = (latent, spec(width, start // width))
    right = (high, spec(high.shape[1], 0)) if last == cols else (latent, spec(EDGE, last // EDGE))
    fields, specs = zip(left, centre, right)
    half = rows // 2
    return pl.pallas_call(
        functools.partial(filter_kernel, start, cols, space_count),
        grid_spec=pltpu.PrefetchScalarGridSpec(
            num_scalar_prefetch=1,
            grid=(hours // lanes,),
            in_specs=[*specs, pl.BlockSpec(weights.shape, lambda i, w: (0, 0))] + anywhere(len(after)),
            out_specs=[pl.BlockSpec((half, width, lanes), lambda i, w: (0, 0, i))] * 2,
            scratch_shapes=[pltpu.VMEM((rows + 2, width + 2 * EDGE, lanes), jnp.float32)] * 2
            + [pltpu.VMEM((rows, width + 2 * EDGE, min(LANES, hours)), jnp.float32)],
        ),
        out_shape=[jax.ShapeDtypeStruct((half, width, hours), jnp.float32)] * 2,
        compiler_params=pltpu.CompilerParams(vmem_limit_bytes=VMEM_LIMIT),
        cost_estimate=LIGHT,
        name="filter",
    )(where, *fields, weights, *after)


def multiply(parts, weights, contract):
    (x_high, x_low), (w_high, w_low) = parts, weights
    dot = functools.partial(
        lax.dot_general,
        dimension_numbers=(((1,), (contract,)), ((), ())),
        preferred_element_type=jnp.float32,
    )
    return dot(x_high, w_high) + (dot(x_low, w_high) + dot(x_high, w_low))


def cut(refs, rows, columns):
    return tuple(ref[rows, columns] for ref in refs)


def blocks(size):
    step = min(FACTOR_BLOCK, size // 2)
    return [slice(i, i + step) for i in range(0, size, step)]


def place_series(source, parts):
    hours = source.shape[2]
    for place in range(2):
        for ref, value in zip(parts, split_bf16(source[place])):
            ref[:, place * hours : (place + 1) * hours] = value


def hours_of(at, size):
    place = at.start // (size // 2)
    return place, slice(at.start - place * size // 2, at.stop - place * size // 2)


def load(weights, buffer, sems):
    return [pltpu.make_async_copy(ref, buffer.at[part], sems.at[part]) for part, ref in enumerate(weights)]


def weight_scratch(size):
    return [pltpu.VMEM((2, size, size), jnp.bfloat16)], [pltpu.SemaphoreType.DMA((2,))]


def begin_kernel(tokens, where_ref, mine, across, *refs):
    refs = refs[tokens:]
    weights, sent, sums, fields, series, middle, held, diagonal, sems, weight_sems = refs[:2], *refs[2:]
    size = held.shape[1]
    core = where_ref[1]
    everything = slice(None)
    series, middle = [series.at[i] for i in range(2)], [middle.at[i] for i in range(2)]
    lower = where_ref[0] == 0
    upper = jnp.logical_not(lower)
    inputs = [
        pltpu.make_async_copy(mine, fields.at[core], sems.at[0]),
        pltpu.make_async_copy(across, fields.at[1 - core], sems.at[1]),
    ]
    hours = size // 2
    forward = [
        pltpu.make_async_copy(fields.at[i], sent.at[:, i * hours : (i + 1) * hours], sems.at[2 + i]) for i in range(2)
    ]
    loads = load(weights, diagonal, weight_sems)
    diagonal = [diagonal.at[i] for i in range(2)]
    start(inputs)
    start(loads)
    wait(inputs)

    @pl.when(upper)
    def _():
        start(forward)

    place_series(fields, series)
    wait(loads)
    for at in blocks(size):
        rows = slice(at.start, size)
        held[:, at] = multiply(cut(series, everything, rows), cut(diagonal, rows, at), 0)

    @pl.when(lower)
    def _():
        output = pltpu.make_async_copy(held, sent, sems.at[4])
        output.start()
        output.wait()

    @pl.when(upper)
    def _():
        for ref, part in zip(middle, split_bf16(held[...])):
            ref[...] = part
        for at in blocks(size):
            columns = slice(0, at.stop)
            held[:, at] = multiply(cut(middle, everything, columns), cut(diagonal, at, columns), 1)
        output = pltpu.make_async_copy(held, sums, sems.at[4])
        output.start()
        wait(forward)
        output.wait()


def begin(where, mine, across, diagonal, after):
    cells, hours = mine.shape
    size = 2 * hours
    operands = [mine, across, *after]
    return pl.pallas_call(
        functools.partial(begin_kernel, len(after)),
        in_specs=[pl.BlockSpec(memory_space=pltpu.SMEM)] + anywhere(len(operands) + 2),
        out_specs=anywhere(2),
        out_shape=[jax.ShapeDtypeStruct((cells, size), jnp.float32)] * 2,
        scratch_shapes=[
            pltpu.VMEM((2, cells, hours), jnp.float32),
            pltpu.VMEM((2, cells, size), jnp.bfloat16),
            pltpu.VMEM((2, cells, size), jnp.bfloat16),
            pltpu.VMEM((cells, size), jnp.float32),
            *weight_scratch(size)[0],
            pltpu.SemaphoreType.DMA((5,)),
            *weight_scratch(size)[1],
        ],
        compiler_params=pltpu.CompilerParams(vmem_limit_bytes=VMEM_LIMIT),
        cost_estimate=LIGHT,
        name="begin",
    )(where, *operands, *diagonal)


def send_hours(core, place, results, targets, sem):
    for target, chosen in zip(targets, (core == place, core != place)):

        @pl.when(chosen)
        def _():
            pltpu.make_async_copy(results.at[place], target, sem).start()


def wait_hours(core, results, targets, sems):
    for place in range(2):
        for target, chosen in zip(targets, (core == place, core != place)):

            @pl.when(chosen)
            def _():
                pltpu.make_async_copy(results.at[place], target, sems[place]).wait()


def end_kernel(tokens, where_ref, sent, sums, arrived, *refs):
    refs = refs[tokens:]
    diagonal_parts, below_parts, targets, refs = refs[:2], refs[2:4], refs[4:6], refs[6:]
    factors, terms, held, series, middle, results, diagonal, below, sems, diagonal_sems, below_sems = refs
    size = factors.shape[1]
    core = where_ref[1]
    everything = slice(None)
    series, middle = [series.at[i] for i in range(2)], [middle.at[i] for i in range(2)]
    lower = where_ref[0] == 0
    upper = jnp.logical_not(lower)

    def inputs(field, term):
        return [
            pltpu.make_async_copy(field, factors, sems.at[0]),
            pltpu.make_async_copy(term, terms, sems.at[1]),
        ]

    before = pltpu.make_async_copy(sums, held, sems.at[2])
    diagonal_loads = load(diagonal_parts, diagonal, diagonal_sems)
    below_loads = load(below_parts, below, below_sems)
    diagonal, below = ([x.at[i] for i in range(2)] for x in (diagonal, below))

    @pl.when(lower)
    def _():
        start(inputs(arrived, sent))

    @pl.when(upper)
    def _():
        start(inputs(sent, arrived))

    start(below_loads)

    @pl.when(lower)
    def _():
        start(diagonal_loads)

    @pl.when(upper)
    def _():
        before.start()

    @pl.when(lower)
    def _():
        wait(inputs(arrived, sent))

    @pl.when(upper)
    def _():
        wait(inputs(sent, arrived))

    for ref, part in zip(series, split_bf16(factors[...])):
        ref[...] = part
    wait(below_loads)
    for at in blocks(size):
        value = terms[:, at] + multiply(cut(series, everything, everything), cut(below, everything, at), 0)
        for ref, part in zip(middle, split_bf16(value)):
            ref[:, at] = part

    @pl.when(lower)
    def _():
        wait(diagonal_loads)

    @pl.when(upper)
    def _():
        before.wait()

    for at in blocks(size):
        columns = slice(0, at.stop)
        place, piece = hours_of(at, size)

        @pl.when(lower)
        def _():
            results[place, :, piece] = multiply(cut(middle, everything, columns), cut(diagonal, at, columns), 1)

        @pl.when(upper)
        def _():
            value = multiply(cut(middle, everything, everything), cut(below, at, everything), 1)
            results[place, :, piece] = held[:, at] + value

        if at.stop == (place + 1) * size // 2:
            send_hours(core, place, results, targets, sems.at[3 + place])
    wait_hours(core, results, targets, [sems.at[3], sems.at[4]])


def end(where, sent, sums, arrived, diagonal, below, after):
    cells, size = sent.shape
    hours = size // 2
    operands = [sent, sums, arrived, *after]
    return pl.pallas_call(
        functools.partial(end_kernel, len(after)),
        in_specs=[pl.BlockSpec(memory_space=pltpu.SMEM)] + anywhere(len(operands) + 4),
        out_specs=anywhere(2),
        out_shape=[jax.ShapeDtypeStruct((cells, hours), jnp.float32)] * 2,
        scratch_shapes=[pltpu.VMEM((cells, size), jnp.float32)] * 3
        + [pltpu.VMEM((2, cells, size), jnp.bfloat16)] * 2
        + [pltpu.VMEM((2, cells, hours), jnp.float32)]
        + weight_scratch(size)[0] * 2
        + [pltpu.SemaphoreType.DMA((5,))]
        + weight_scratch(size)[1] * 2,
        compiler_params=pltpu.CompilerParams(vmem_limit_bytes=VMEM_LIMIT),
        cost_estimate=LIGHT,
        name="end",
    )(where, *operands, *diagonal, *below)


def join_kernel(count, *refs):
    out, held, sems = refs[-3:]
    first = 0
    group = []
    for i, ref in enumerate(refs[:count]):
        group.append(pltpu.make_async_copy(ref, held.at[pl.ds(first, ref.shape[0])], sems.at[i]))
        first += ref.shape[0]
    start(group)
    wait(group)
    output = pltpu.make_async_copy(held, out, sems.at[count])
    output.start()
    output.wait()


def join(pieces, after):
    shape = (sum(x.shape[0] for x in pieces), *pieces[0].shape[1:])
    return pl.pallas_call(
        functools.partial(join_kernel, len(pieces)),
        in_specs=anywhere(len(pieces) + len(after)),
        out_specs=pl.BlockSpec(memory_space=pl.ANY),
        out_shape=jax.ShapeDtypeStruct(shape, pieces[0].dtype),
        scratch_shapes=[pltpu.VMEM(shape, pieces[0].dtype), pltpu.SemaphoreType.DMA((len(pieces) + 1,))],
        compiler_params=pltpu.CompilerParams(vmem_limit_bytes=VMEM_LIMIT),
        cost_estimate=LIGHT,
        name="join",
    )(*pieces, *after)


def finish_kernel(where_ref, step_ref, own, beside, latent_ref, events_ref, base_ref, draw_ref, *refs):
    gradient_ref, proposal_ref = refs[-2:]
    latent = latent_ref[...]
    spread = jnp.sqrt(jnp.full((1, 1, latent.shape[2]), 2.0 * step_ref[0]))
    data = events_ref[...].astype(jnp.float32) - jnp.exp(base_ref[...] + latent)
    for turn, prior in enumerate((own, beside)):

        @pl.when(pl.program_id(0) == turn)
        def _():
            slope = data - prior[...]
            gradient_ref[...] = slope
            proposal_ref[...] = latent + step_ref[0] * slope + spread * draw_ref[...]


def finish(where, steps, priors, fields, start, width, outs, after):
    rows, cols, hours = fields[0].shape
    half = rows // 2
    shape = (half, width, hours)
    held = [prior.reshape(shape) for prior in priors]
    held_spec = pl.BlockSpec(shape, lambda i, w, s: (0, 0, 0))
    field_spec = pl.BlockSpec(shape, lambda i, w, s: ((w[1] + i) % 2, start // width, 0))
    out = jax.ShapeDtypeStruct((rows, cols, hours), jnp.float32)
    return pl.pallas_call(
        finish_kernel,
        grid_spec=pltpu.PrefetchScalarGridSpec(
            num_scalar_prefetch=2,
            grid=(2,),
            in_specs=[held_spec] * 2 + [field_spec] * 4 + anywhere(len(outs) + len(after)),
            out_specs=[field_spec] * 2,
        ),
        out_shape=[out, out],
        input_output_aliases={8 + i: i for i in range(len(outs))},
        compiler_params=pltpu.CompilerParams(vmem_limit_bytes=VMEM_LIMIT),
        cost_estimate=LIGHT,
        name="finish",
    )(where, steps, *held, *fields, *outs, *after)


def column_plan(cols):
    starts = list(range(0, cols, WIDTH))
    return [(s, WIDTH) for s in starts[1:-1] + [starts[0], starts[-1]]]


def local(latent, events, log_base, innovation, kappa_sq, chol_factor, step_size):
    rows, cols, hours = latent.shape
    place = lax.axis_index("tm")
    upper, core = place // 2, place % 2
    space = lax.axis_index("space")
    space_count = lax.axis_size("space")
    where = jnp.stack([upper, core, space]).astype(jnp.int32)

    def beside(x):
        return lax.ppermute(x, "tm", [(0, 1), (1, 0), (2, 3), (3, 2)])

    def exchange(x):
        return lax.ppermute(x, "tm", [(0, 2), (1, 3), (2, 0), (3, 1)])

    across_core = beside(chol_factor)
    forward = [(i, i + 1) for i in range(space_count - 1)]
    backward = [(i + 1, i) for i in range(space_count - 1)]
    halos = (
        lax.ppermute(latent[:, cols - 2 :], "space", forward),
        lax.ppermute(latent[:, :2], "space", backward),
    )
    padded = jnp.pad(kappa_sq, ((0, 0), (EDGE, EDGE))) + 4.0
    weights = lax.dynamic_slice(padded, (jnp.int32(0), space * cols), (rows, cols + 2 * EDGE)).T
    plan = column_plan(cols)
    fields = (latent, events, log_base, innovation)
    mine, others, sent, sums, arrived, totals = ({} for _ in range(6))

    def make_field(k, after):
        made = filtered(where, latent, halos, weights, *plan[k], space_count, after)
        mine[k], away = (x.reshape(-1, hours) for x in made)
        others[k] = beside(away)

    def begin_chunk(k, after):
        sent[k], sums[k] = begin(where, mine[k], others[k], diagonal, after)
        arrived[k] = exchange(sent[k])

    def end_chunk(k, after):
        own, across = end(where, sent[k], sums[k], arrived[k], diagonal, below, after)
        totals[k] = own, beside(across)

    def finish_chunk(k, after):
        return finish(where, step_size, totals[k], fields, *plan[k], outs, after)

    order = [0]

    def double(x):
        bit = space_count // 2 // len(order)
        order.extend([i ^ bit for i in order])
        return lax.ppermute(x, "space", [(i, i ^ bit) for i in range(space_count)])

    outs = []
    share = 2 * hours // space_count
    slab = lax.dynamic_slice(chol_factor, (2 * hours + space * share, jnp.int32(0)), (share, hours))
    held = lax.ppermute(slab, "tm", [(0, 2), (1, 3)])[None]
    received = double(held)
    make_field(0, [])
    diagonal = split_diagonal(where, chol_factor, across_core, [mine[0]])
    begin_chunk(0, [])
    held = join([held, received], [sent[0]])
    received = double(held)
    make_field(1, [held])
    make_field(2, [mine[1], *halos])
    held = join([held, received], [mine[2]])
    received = double(held)
    begin_chunk(1, [held])
    make_field(3, [sent[1]])
    begin_chunk(2, [mine[3]])
    received = join([received], [sent[2], arrived[0]])
    begin_chunk(3, [received])
    gathered = [held, received, beside(held), beside(received)]
    order = space.astype(jnp.int32) ^ jnp.array(order, jnp.int32)
    below = split_below(where, order, chol_factor, across_core, gathered, [sent[3]])
    end_chunk(0, [])
    end_chunk(1, [totals[0][0]])
    end_chunk(2, [totals[1][0]])
    outs = finish_chunk(0, [totals[2][0]])
    outs = finish_chunk(1, [])
    outs = finish_chunk(2, [])
    end_chunk(3, [outs[0]])
    return finish_chunk(3, [])


def plain(latent, events, log_base, innovation, kappa_sq, chol_factor, step_size):
    rows, cols, hours = latent.shape
    space = lax.axis_index("space")
    count = lax.axis_size("space")
    forward = [(i, i + 1) for i in range(count - 1)]
    backward = [(i + 1, i) for i in range(count - 1)]
    kappa = lax.dynamic_slice(kappa_sq, (jnp.int32(0), space * cols), (rows, cols))

    def operate(field):
        low = lax.ppermute(field[:, -1:], "space", forward)
        high = lax.ppermute(field[:, :1], "space", backward)
        row_padded = jnp.pad(field, ((1, 1), (0, 0), (0, 0)))
        wide = jnp.concatenate([low, field, high], axis=1)
        beside = row_padded[2:] + row_padded[:-2] + wide[:, 2:] + wide[:, :-2]
        return (kappa[:, :, None] + 4.0) * field - beside

    dot = functools.partial(lax.dot_general, precision=lax.Precision.HIGHEST, preferred_element_type=jnp.float32)
    series = operate(operate(latent)).reshape(rows * cols, hours)
    projected = dot(lax.all_gather(series, "tm", axis=1, tiled=True), chol_factor, (((1,), (0,)), ((), ())))
    sums = dot(chol_factor, projected, (((1,), (1,)), ((), ())))
    by_hour = lax.psum_scatter(sums, "tm", scatter_dimension=0, tiled=True)
    prior = by_hour.T.reshape(rows, cols, hours)
    gradient = events.astype(jnp.float32) - jnp.exp(log_base + latent) - prior
    proposal = latent + step_size[0] * gradient + jnp.sqrt(2.0 * step_size[0]) * innovation
    return gradient, proposal


def solution(mesh):
    in_specs = (
        P(None, "space", "tm"),
        P(None, "space", "tm"),
        P(None, "space", "tm"),
        P(None, "space", "tm"),
        P(),
        P(None, "tm"),
        P(),
    )
    out_specs = (P(None, "space", "tm"), P(None, "space", "tm"))
    body = local if mesh.shape["tm"] == 4 and mesh.shape["space"] == 8 else plain
    return jax.shard_map(body, mesh=mesh, in_specs=in_specs, out_specs=out_specs, check_vma=False)
```

```python
import functools

import jax
import jax.numpy as jnp
from jax import lax
from jax.experimental import pallas as pl
from jax.experimental.pallas import tpu as pltpu
from jax.sharding import PartitionSpec as P

EDGE = 8
LANES = 128
CHUNKS = ((32, 32), (64, 32), (0, 32), (96, 32))
ORDER = "F0 D B0 F1 F2 J1 B1 F3 J2 B2 B3 J3 S E0 E1 E2 f0 f1 f2 E3 f3"
PINS = {"F2": "halo", "J2": "Y0", "B0": "slab", "J3": "Y1"}
FACTOR_BLOCK = 256
VMEM_LIMIT = 60 * 1024 * 1024
LIGHT = pl.CostEstimate(flops=0, bytes_accessed=4096, transcendentals=0)


def split_bf16(x):
    high = x.astype(jnp.bfloat16)
    return high, (x - high.astype(jnp.float32)).astype(jnp.bfloat16)


def anywhere(count):
    return [pl.BlockSpec(memory_space=pl.ANY)] * count


def in_vmem(count):
    return [pl.BlockSpec(memory_space=pltpu.VMEM)] * count


def start(group):
    for copy in group:
        copy.start()


def wait(group):
    for copy in group:
        copy.wait()


def split_rows(where_ref, own, beside, first, held, sems, targets):
    size, width = targets[0].shape[0], own.shape[1]
    step = held.shape[2]
    places = (where_ref[1], 1 - where_ref[1])
    groups = [
        [
            pltpu.make_async_copy(source.at[pl.ds(first + row, step)], held.at[i, j], sems.at[i, j])
            for j, source in enumerate((own, beside))
        ]
        for i, row in enumerate(range(0, size, step))
    ]
    for copies in groups:
        start(copies)
    for i, copies in enumerate(groups):
        wait(copies)
        for j, place in enumerate(places):
            store_columns(targets, place, slice(i * step, (i + 1) * step), held[i, j])


def store_columns(targets, place, rows, values):
    width = values.shape[1]
    at = pl.ds(pl.multiple_of(place * width, width), width)
    for ref, value in zip(targets, split_bf16(values)):
        ref[rows, at] = value


def diagonal_kernel(tokens, where_ref, own, beside, *refs):
    *targets, held, sems = refs[tokens:]
    split_rows(where_ref, own, beside, where_ref[0] * targets[0].shape[0], held, sems, targets)


def split_scratch(size, width):
    step = min(FACTOR_BLOCK, size)
    return [pltpu.VMEM((size // step, 2, step, width), jnp.float32), pltpu.SemaphoreType.DMA((size // step, 2))]


def split_diagonal(where, own, beside, after):
    hours, width = own.shape
    half = hours // 2
    return pl.pallas_call(
        functools.partial(diagonal_kernel, len(after)),
        in_specs=[pl.BlockSpec(memory_space=pltpu.SMEM)] + anywhere(2 + len(after)),
        out_specs=in_vmem(2),
        out_shape=[jax.ShapeDtypeStruct((half, 2 * width), jnp.bfloat16)] * 2,
        scratch_shapes=split_scratch(half, width),
        compiler_params=pltpu.CompilerParams(vmem_limit_bytes=VMEM_LIMIT),
        cost_estimate=LIGHT,
        name="split_diagonal",
    )(where, own, beside, *after)


def below_kernel(tokens, where_ref, order_ref, own, beside, *refs):
    gathered, refs = refs[:4], refs[4 + tokens :]
    *targets, held, sems, parts, part_sems = refs
    size = targets[0].shape[0]

    @pl.when(where_ref[0] == 0)
    def _():
        split_rows(where_ref, own, beside, size, held, sems, targets)

    @pl.when(where_ref[0] != 0)
    def _():
        count, step = gathered[0].shape[:2]
        copies = [pltpu.make_async_copy(ref, parts.at[i], part_sems.at[i]) for i, ref in enumerate(gathered)]
        start(copies)
        for i, copy in enumerate(copies):
            copy.wait()
            place = where_ref[1] if i < 2 else 1 - where_ref[1]
            for j in range(count):
                rows = pl.ds(pl.multiple_of(order_ref[i % 2 * count + j] * step, step), step)
                store_columns(targets, place, rows, parts[i, j])


def split_below(where, order, own, beside, gathered, after):
    hours, width = own.shape
    half = hours // 2
    return pl.pallas_call(
        functools.partial(below_kernel, len(after)),
        in_specs=[pl.BlockSpec(memory_space=pltpu.SMEM)] * 2 + anywhere(6 + len(after)),
        out_specs=in_vmem(2),
        out_shape=[jax.ShapeDtypeStruct((half, 2 * width), jnp.bfloat16)] * 2,
        scratch_shapes=split_scratch(half, width)
        + [pltpu.VMEM((4, *gathered[0].shape), jnp.float32), pltpu.SemaphoreType.DMA((4,))],
        compiler_params=pltpu.CompilerParams(vmem_limit_bytes=VMEM_LIMIT),
        cost_estimate=LIGHT,
        name="split_below",
    )(where, order, own, beside, *gathered, *after)


def filter_kernel(first_col, cols, space_count, where_ref, left, centre, right, weight_ref, *refs):
    mine_ref, other_ref, wide, once, scale = refs[-5:]
    rows, width, lanes = centre.shape
    around = width + 2 * EDGE
    core, space = where_ref[1], where_ref[2]
    zero = jnp.zeros((around, lanes), jnp.float32)
    for ref in (wide, once):
        ref[0] = zero
        ref[rows + 1] = zero
    wide[1 : rows + 1, EDGE - left.shape[1] : EDGE, :] = left[...]
    wide[1 : rows + 1, EDGE : EDGE + width, :] = centre[...]
    wide[1 : rows + 1, EDGE + width : EDGE + width + right.shape[1], :] = right[...]

    @pl.when(pl.program_id(0) == 0)
    def _():
        for row in range(rows):
            scale[row] = jnp.broadcast_to(weight_ref[first_col : first_col + around, row : row + 1], scale.shape[1:])

    strip = scale.shape[2]
    column = space * cols + first_col - EDGE + lax.broadcasted_iota(jnp.int32, (around, strip), 0)
    inside = (column >= 0) & (column < space_count * cols)

    def operate(source, row, at):
        x = source[row + 1, :, at]
        beside = source[row, :, at] + source[row + 2, :, at] + pltpu.roll(x, 1, 0) + pltpu.roll(x, around - 1, 0)
        return scale[row] * x - beside

    for place in range(lanes // strip):
        at = slice(place * strip, (place + 1) * strip)

        def first(row, carry):
            value = operate(wide, row, at)
            if first_col == 0 or first_col + width == cols:
                value = jnp.where(inside, value, 0.0)
            once[row + 1, :, at] = value
            return carry

        def second(row, carry):
            mine_ref[row, :, at] = operate(once, row + core * (rows // 2), at)[EDGE : EDGE + width]
            other_ref[row, :, at] = operate(once, row + (1 - core) * (rows // 2), at)[EDGE : EDGE + width]
            return carry

        lax.fori_loop(0, rows, first, 0, unroll=4)
        lax.fori_loop(0, rows // 2, second, 0, unroll=2)


def filtered(where, latent, halos, weights, start, width, space_count, after):
    rows, cols, hours = latent.shape
    lanes = min(2 * LANES, hours)
    last = start + width

    def spec(columns, index):
        return pl.BlockSpec((rows, columns, lanes), lambda i, w: (0, index, i))

    low, high = halos
    left = (low, spec(low.shape[1], 0)) if start == 0 else (latent, spec(EDGE, start // EDGE - 1))
    centre = (latent, spec(width, start // width))
    right = (high, spec(high.shape[1], 0)) if last == cols else (latent, spec(EDGE, last // EDGE))
    fields, specs = zip(left, centre, right)
    half = rows // 2
    return pl.pallas_call(
        functools.partial(filter_kernel, start, cols, space_count),
        grid_spec=pltpu.PrefetchScalarGridSpec(
            num_scalar_prefetch=1,
            grid=(hours // lanes,),
            in_specs=[*specs, pl.BlockSpec(weights.shape, lambda i, w: (0, 0))] + anywhere(len(after)),
            out_specs=[pl.BlockSpec((half, width, lanes), lambda i, w: (0, 0, i))] * 2,
            scratch_shapes=[pltpu.VMEM((rows + 2, width + 2 * EDGE, lanes), jnp.float32)] * 2
            + [pltpu.VMEM((rows, width + 2 * EDGE, min(LANES, hours)), jnp.float32)],
        ),
        out_shape=[jax.ShapeDtypeStruct((half, width, hours), jnp.float32)] * 2,
        compiler_params=pltpu.CompilerParams(vmem_limit_bytes=VMEM_LIMIT),
        cost_estimate=LIGHT,
        name="filter",
    )(where, *fields, weights, *after)


def multiply(parts, weights, contract):
    (x_high, x_low), (w_high, w_low) = parts, weights
    dot = functools.partial(
        lax.dot_general,
        dimension_numbers=(((1,), (contract,)), ((), ())),
        preferred_element_type=jnp.float32,
    )
    return dot(x_high, w_high) + (dot(x_low, w_high) + dot(x_high, w_low))


def cut(refs, rows, columns):
    return tuple(ref[rows, columns] for ref in refs)


def blocks(size):
    step = min(FACTOR_BLOCK, size // 2)
    return [slice(i, i + step) for i in range(0, size, step)]


def place_series(source, parts):
    hours = source.shape[2]
    for place in range(2):
        for ref, value in zip(parts, split_bf16(source[place])):
            ref[:, place * hours : (place + 1) * hours] = value


def hours_of(at, size):
    place = at.start // (size // 2)
    return place, slice(at.start - place * size // 2, at.stop - place * size // 2)


def load(weights, buffer, sems):
    return [pltpu.make_async_copy(ref, buffer.at[part], sems.at[part]) for part, ref in enumerate(weights)]


def weight_scratch(size):
    return [pltpu.VMEM((2, size, size), jnp.bfloat16)], [pltpu.SemaphoreType.DMA((2,))]


def begin_kernel(tokens, where_ref, mine, across, *refs):
    refs = refs[tokens:]
    weights, sent, sums, fields, series, middle, held, diagonal, sems, weight_sems = refs[:2], *refs[2:]
    size = held.shape[1]
    core = where_ref[1]
    everything = slice(None)
    series, middle = [series.at[i] for i in range(2)], [middle.at[i] for i in range(2)]
    lower = where_ref[0] == 0
    upper = jnp.logical_not(lower)
    inputs = [
        pltpu.make_async_copy(mine, fields.at[core], sems.at[0]),
        pltpu.make_async_copy(across, fields.at[1 - core], sems.at[1]),
    ]
    hours = size // 2
    forward = [
        pltpu.make_async_copy(fields.at[i], sent.at[:, i * hours : (i + 1) * hours], sems.at[2 + i]) for i in range(2)
    ]
    loads = load(weights, diagonal, weight_sems)
    diagonal = [diagonal.at[i] for i in range(2)]
    start(inputs)
    start(loads)
    wait(inputs)

    @pl.when(upper)
    def _():
        start(forward)

    place_series(fields, series)
    wait(loads)
    for at in blocks(size):
        rows = slice(at.start, size)
        held[:, at] = multiply(cut(series, everything, rows), cut(diagonal, rows, at), 0)

    @pl.when(lower)
    def _():
        output = pltpu.make_async_copy(held, sent, sems.at[4])
        output.start()
        output.wait()

    @pl.when(upper)
    def _():
        for ref, part in zip(middle, split_bf16(held[...])):
            ref[...] = part
        for at in blocks(size):
            columns = slice(0, at.stop)
            held[:, at] = multiply(cut(middle, everything, columns), cut(diagonal, at, columns), 1)
        output = pltpu.make_async_copy(held, sums, sems.at[4])
        output.start()
        wait(forward)
        output.wait()


def begin(where, mine, across, diagonal, after):
    cells, hours = mine.shape
    size = 2 * hours
    operands = [mine, across, *after]
    return pl.pallas_call(
        functools.partial(begin_kernel, len(after)),
        in_specs=[pl.BlockSpec(memory_space=pltpu.SMEM)] + anywhere(len(operands) + 2),
        out_specs=anywhere(2),
        out_shape=[jax.ShapeDtypeStruct((cells, size), jnp.float32)] * 2,
        scratch_shapes=[
            pltpu.VMEM((2, cells, hours), jnp.float32),
            pltpu.VMEM((2, cells, size), jnp.bfloat16),
            pltpu.VMEM((2, cells, size), jnp.bfloat16),
            pltpu.VMEM((cells, size), jnp.float32),
            *weight_scratch(size)[0],
            pltpu.SemaphoreType.DMA((5,)),
            *weight_scratch(size)[1],
        ],
        compiler_params=pltpu.CompilerParams(vmem_limit_bytes=VMEM_LIMIT),
        cost_estimate=LIGHT,
        name="begin",
    )(where, *operands, *diagonal)


def send_hours(core, place, results, targets, sem):
    for target, chosen in zip(targets, (core == place, core != place)):

        @pl.when(chosen)
        def _():
            pltpu.make_async_copy(results.at[place], target, sem).start()


def wait_hours(core, results, targets, sems):
    for place in range(2):
        for target, chosen in zip(targets, (core == place, core != place)):

            @pl.when(chosen)
            def _():
                pltpu.make_async_copy(results.at[place], target, sems[place]).wait()


def end_kernel(tokens, where_ref, sent, sums, arrived, *refs):
    refs = refs[tokens:]
    diagonal_parts, below_parts, targets, refs = refs[:2], refs[2:4], refs[4:6], refs[6:]
    factors, terms, held, series, middle, results, diagonal, below, sems, diagonal_sems, below_sems = refs
    size = factors.shape[1]
    core = where_ref[1]
    everything = slice(None)
    series, middle = [series.at[i] for i in range(2)], [middle.at[i] for i in range(2)]
    lower = where_ref[0] == 0
    upper = jnp.logical_not(lower)

    def inputs(field, term):
        return [
            pltpu.make_async_copy(field, factors, sems.at[0]),
            pltpu.make_async_copy(term, terms, sems.at[1]),
        ]

    before = pltpu.make_async_copy(sums, held, sems.at[2])
    diagonal_loads = load(diagonal_parts, diagonal, diagonal_sems)
    below_loads = load(below_parts, below, below_sems)
    diagonal, below = ([x.at[i] for i in range(2)] for x in (diagonal, below))

    @pl.when(lower)
    def _():
        start(inputs(arrived, sent))

    @pl.when(upper)
    def _():
        start(inputs(sent, arrived))

    start(below_loads)

    @pl.when(lower)
    def _():
        start(diagonal_loads)

    @pl.when(upper)
    def _():
        before.start()

    @pl.when(lower)
    def _():
        wait(inputs(arrived, sent))

    @pl.when(upper)
    def _():
        wait(inputs(sent, arrived))

    for ref, part in zip(series, split_bf16(factors[...])):
        ref[...] = part
    wait(below_loads)
    for at in blocks(size):
        value = terms[:, at] + multiply(cut(series, everything, everything), cut(below, everything, at), 0)
        for ref, part in zip(middle, split_bf16(value)):
            ref[:, at] = part

    @pl.when(lower)
    def _():
        wait(diagonal_loads)

    @pl.when(upper)
    def _():
        before.wait()

    for at in blocks(size):
        columns = slice(0, at.stop)
        place, piece = hours_of(at, size)

        @pl.when(lower)
        def _():
            results[place, :, piece] = multiply(cut(middle, everything, columns), cut(diagonal, at, columns), 1)

        @pl.when(upper)
        def _():
            value = multiply(cut(middle, everything, everything), cut(below, at, everything), 1)
            results[place, :, piece] = held[:, at] + value

        if at.stop == (place + 1) * size // 2:
            send_hours(core, place, results, targets, sems.at[3 + place])
    wait_hours(core, results, targets, [sems.at[3], sems.at[4]])


def end(where, sent, sums, arrived, diagonal, below, after):
    cells, size = sent.shape
    hours = size // 2
    operands = [sent, sums, arrived, *after]
    return pl.pallas_call(
        functools.partial(end_kernel, len(after)),
        in_specs=[pl.BlockSpec(memory_space=pltpu.SMEM)] + anywhere(len(operands) + 4),
        out_specs=anywhere(2),
        out_shape=[jax.ShapeDtypeStruct((cells, hours), jnp.float32)] * 2,
        scratch_shapes=[pltpu.VMEM((cells, size), jnp.float32)] * 3
        + [pltpu.VMEM((2, cells, size), jnp.bfloat16)] * 2
        + [pltpu.VMEM((2, cells, hours), jnp.float32)]
        + weight_scratch(size)[0] * 2
        + [pltpu.SemaphoreType.DMA((5,))]
        + weight_scratch(size)[1] * 2,
        compiler_params=pltpu.CompilerParams(vmem_limit_bytes=VMEM_LIMIT),
        cost_estimate=LIGHT,
        name="end",
    )(where, *operands, *diagonal, *below)


def join_kernel(count, *refs):
    out, held, sems = refs[-3:]
    first = 0
    group = []
    for i, ref in enumerate(refs[:count]):
        group.append(pltpu.make_async_copy(ref, held.at[pl.ds(first, ref.shape[0])], sems.at[i]))
        first += ref.shape[0]
    start(group)
    wait(group)
    output = pltpu.make_async_copy(held, out, sems.at[count])
    output.start()
    output.wait()


def join(pieces, after):
    shape = (sum(x.shape[0] for x in pieces), *pieces[0].shape[1:])
    return pl.pallas_call(
        functools.partial(join_kernel, len(pieces)),
        in_specs=anywhere(len(pieces) + len(after)),
        out_specs=pl.BlockSpec(memory_space=pl.ANY),
        out_shape=jax.ShapeDtypeStruct(shape, pieces[0].dtype),
        scratch_shapes=[pltpu.VMEM(shape, pieces[0].dtype), pltpu.SemaphoreType.DMA((len(pieces) + 1,))],
        compiler_params=pltpu.CompilerParams(vmem_limit_bytes=VMEM_LIMIT),
        cost_estimate=LIGHT,
        name="join",
    )(*pieces, *after)


def finish_kernel(turns, where_ref, step_ref, own, beside, latent_ref, events_ref, base_ref, draw_ref, *refs):
    gradient_ref, proposal_ref = refs[-2:]
    latent = latent_ref[...]
    spread = jnp.sqrt(jnp.full((1, 1, latent.shape[2]), 2.0 * step_ref[0]))
    data = events_ref[...].astype(jnp.float32) - jnp.exp(base_ref[...] + latent)
    for i, turn in enumerate(turns):
        prior = (own, beside)[turn]

        @pl.when(pl.program_id(0) == i)
        def _():
            slope = data - prior[...]
            gradient_ref[...] = slope
            proposal_ref[...] = latent + step_ref[0] * slope + spread * draw_ref[...]


def finish(where, steps, priors, fields, start, width, outs, after, turns):
    rows, cols, hours = fields[0].shape
    half = rows // 2
    shape = (half, width, hours)
    held = [prior.reshape(shape) for prior in priors]
    held_spec = pl.BlockSpec(shape, lambda i, w, s: (0, 0, 0))
    field_spec = pl.BlockSpec(shape, lambda i, w, s: ((w[1] + i + turns[0]) % 2, start // width, 0))
    out = jax.ShapeDtypeStruct((rows, cols, hours), jnp.float32)
    return pl.pallas_call(
        functools.partial(finish_kernel, turns),
        grid_spec=pltpu.PrefetchScalarGridSpec(
            num_scalar_prefetch=2,
            grid=(len(turns),),
            in_specs=[held_spec] * 2 + [field_spec] * 4 + anywhere(len(outs) + len(after)),
            out_specs=[field_spec] * 2,
        ),
        out_shape=[out, out],
        input_output_aliases={8 + i: i for i in range(len(outs))},
        compiler_params=pltpu.CompilerParams(vmem_limit_bytes=VMEM_LIMIT),
        cost_estimate=LIGHT,
        name="finish",
    )(where, steps, *held, *fields, *outs, *after)


def local(latent, events, log_base, innovation, kappa_sq, chol_factor, step_size):
    rows, cols, hours = latent.shape
    place = lax.axis_index("tm")
    upper, core = place // 2, place % 2
    space = lax.axis_index("space")
    space_count = lax.axis_size("space")
    where = jnp.stack([upper, core, space]).astype(jnp.int32)

    def beside(x):
        return lax.ppermute(x, "tm", [(0, 1), (1, 0), (2, 3), (3, 2)])

    def exchange(x):
        return lax.ppermute(x, "tm", [(0, 2), (1, 3), (2, 0), (3, 1)])

    across_core = beside(chol_factor)
    forward = [(i, i + 1) for i in range(space_count - 1)]
    backward = [(i + 1, i) for i in range(space_count - 1)]
    halos = (
        lax.ppermute(latent[:, cols - 2 :], "space", forward),
        lax.ppermute(latent[:, :2], "space", backward),
    )
    padded = jnp.pad(kappa_sq, ((0, 0), (EDGE, EDGE))) + 4.0
    weights = lax.dynamic_slice(padded, (jnp.int32(0), space * cols), (rows, cols + 2 * EDGE)).T
    fields = (latent, events, log_base, innovation)
    mine, others, sent, sums, arrived, totals = ({} for _ in range(6))

    share = 2 * hours // space_count
    slab = lax.dynamic_slice(chol_factor, (2 * hours + space * share, jnp.int32(0)), (share, hours))
    held = lax.ppermute(slab, "tm", [(0, 2), (1, 3)])[None]
    order = [0]

    def double(x):
        bit = space_count // 2 // len(order)
        order.extend([i ^ bit for i in order])
        return lax.ppermute(x, "space", [(i, i ^ bit) for i in range(space_count)])

    received = double(held)
    transfers = {"slab": [held], "halo": [*halos]}
    token, outs = [], []
    for name in ORDER.split():
        kind, k = name[0], int(name[1:] or 0)
        after = token + [x for pin in PINS.get(name, "").split() for x in transfers[pin]]
        if kind == "F":
            made = filtered(where, latent, halos, weights, *CHUNKS[k], space_count, after)
            mine[k], away = (x.reshape(-1, hours) for x in made)
            others[k] = beside(away)
            token = [mine[k]]
        elif kind == "D":
            diagonal = split_diagonal(where, chol_factor, across_core, after)
            token = [diagonal[0]]
        elif kind == "B":
            sent[k], sums[k] = begin(where, mine[k], others[k], diagonal, after)
            arrived[k] = exchange(sent[k])
            transfers["Y" + name[1:]] = [arrived[k]]
            token = [sent[k]]
        elif kind == "J" and k < 3:
            held = join([held, received], after)
            received = double(held)
            token = [held]
        elif kind == "J":
            received = join([received], after)
            token = [received]
        elif kind == "S":
            gathered = [held, received, beside(held), beside(received)]
            order = space.astype(jnp.int32) ^ jnp.array(order, jnp.int32)
            below = split_below(where, order, chol_factor, across_core, gathered, after)
            token = [below[0]]
        elif kind == "E":
            own, across = end(where, sent[k], sums[k], arrived[k], diagonal, below, after)
            totals[k] = own, beside(across)
            token = [own]
        else:
            own, across = totals[k]
            turns = {"f": (0, 1), "g": (0,), "h": (1,)}[kind]
            priors = (own, own) if kind == "g" else (own, across)
            after = [x for x in after if not any(x is y for y in outs)]
            outs = finish(where, step_size, priors, fields, *CHUNKS[k], outs, after, turns)
            token = [outs[0]]
    return outs


def plain(latent, events, log_base, innovation, kappa_sq, chol_factor, step_size):
    rows, cols, hours = latent.shape
    space = lax.axis_index("space")
    count = lax.axis_size("space")
    forward = [(i, i + 1) for i in range(count - 1)]
    backward = [(i + 1, i) for i in range(count - 1)]
    kappa = lax.dynamic_slice(kappa_sq, (jnp.int32(0), space * cols), (rows, cols))

    def operate(field):
        low = lax.ppermute(field[:, -1:], "space", forward)
        high = lax.ppermute(field[:, :1], "space", backward)
        row_padded = jnp.pad(field, ((1, 1), (0, 0), (0, 0)))
        wide = jnp.concatenate([low, field, high], axis=1)
        beside = row_padded[2:] + row_padded[:-2] + wide[:, 2:] + wide[:, :-2]
        return (kappa[:, :, None] + 4.0) * field - beside

    dot = functools.partial(lax.dot_general, precision=lax.Precision.HIGHEST, preferred_element_type=jnp.float32)
    series = operate(operate(latent)).reshape(rows * cols, hours)
    projected = dot(lax.all_gather(series, "tm", axis=1, tiled=True), chol_factor, (((1,), (0,)), ((), ())))
    sums = dot(chol_factor, projected, (((1,), (1,)), ((), ())))
    by_hour = lax.psum_scatter(sums, "tm", scatter_dimension=0, tiled=True)
    prior = by_hour.T.reshape(rows, cols, hours)
    gradient = events.astype(jnp.float32) - jnp.exp(log_base + latent) - prior
    proposal = latent + step_size[0] * gradient + jnp.sqrt(2.0 * step_size[0]) * innovation
    return gradient, proposal


def solution(mesh):
    in_specs = (
        P(None, "space", "tm"),
        P(None, "space", "tm"),
        P(None, "space", "tm"),
        P(None, "space", "tm"),
        P(),
        P(None, "tm"),
        P(),
    )
    out_specs = (P(None, "space", "tm"), P(None, "space", "tm"))
    body = local if mesh.shape["tm"] == 4 and mesh.shape["space"] == 8 else plain
    return jax.shard_map(body, mesh=mesh, in_specs=in_specs, out_specs=out_specs, check_vma=False)
```

```python
import functools

import jax
import jax.numpy as jnp
from jax import lax
from jax.experimental import pallas as pl
from jax.experimental.pallas import tpu as pltpu
from jax.sharding import PartitionSpec as P

EDGE = 8
LANES = 128
CHUNKS = ((32, 32), (64, 32), (0, 32), (96, 32))
ORDER = ("F0", "D", "B0", "F1", "B1", "J1", "F2", "J2", "B2", "F3", "B3", "J3", "S", "E0", "E1", "E2", "f0", "f1", "f2", "E3", "f3")
PINS = {"F2": ("halo",), "J2": ("Y0",), "B0": ("slab",), "J3": ("Y1",)}
FACTOR_BLOCK = 256
VMEM_LIMIT = 63 * 1024 * 1024
LIGHT = pl.CostEstimate(flops=0, bytes_accessed=4096, transcendentals=0)


def split_bf16(x):
    high = x.astype(jnp.bfloat16)
    return high, (x - high.astype(jnp.float32)).astype(jnp.bfloat16)


def anywhere(count):
    return [pl.BlockSpec(memory_space=pl.ANY)] * count


def in_vmem(count):
    return [pl.BlockSpec(memory_space=pltpu.VMEM)] * count


def start(group):
    for copy in group:
        copy.start()


def wait(group):
    for copy in group:
        copy.wait()


def split_rows(where_ref, own, beside, first, held, sems, targets):
    size, width = targets[0].shape[0], own.shape[1]
    step = held.shape[2]
    places = (where_ref[1], 1 - where_ref[1])
    groups = [
        [
            pltpu.make_async_copy(source.at[pl.ds(first + row, step)], held.at[i, j], sems.at[i, j])
            for j, source in enumerate((own, beside))
        ]
        for i, row in enumerate(range(0, size, step))
    ]
    for copies in groups:
        start(copies)
    for i, copies in enumerate(groups):
        wait(copies)
        for j, place in enumerate(places):
            store_columns(targets, place, slice(i * step, (i + 1) * step), held[i, j])


def store_columns(targets, place, rows, values):
    width = values.shape[1]
    at = pl.ds(pl.multiple_of(place * width, width), width)
    for ref, value in zip(targets, split_bf16(values)):
        ref[rows, at] = value


def diagonal_kernel(tokens, where_ref, own, beside, *refs):
    *targets, held, sems = refs[tokens:]
    split_rows(where_ref, own, beside, where_ref[0] * targets[0].shape[0], held, sems, targets)


def split_scratch(size, width):
    step = min(FACTOR_BLOCK, size)
    return [pltpu.VMEM((size // step, 2, step, width), jnp.float32), pltpu.SemaphoreType.DMA((size // step, 2))]


def split_diagonal(where, own, beside, after):
    hours, width = own.shape
    half = hours // 2
    return pl.pallas_call(
        functools.partial(diagonal_kernel, len(after)),
        in_specs=[pl.BlockSpec(memory_space=pltpu.SMEM)] + anywhere(2 + len(after)),
        out_specs=in_vmem(2),
        out_shape=[jax.ShapeDtypeStruct((half, 2 * width), jnp.bfloat16)] * 2,
        scratch_shapes=split_scratch(half, width),
        compiler_params=pltpu.CompilerParams(vmem_limit_bytes=VMEM_LIMIT),
        cost_estimate=LIGHT,
        name="split_diagonal",
    )(where, own, beside, *after)


def below_kernel(tokens, where_ref, order_ref, own, beside, *refs):
    gathered, refs = refs[:4], refs[4 + tokens :]
    *targets, held, sems, parts, part_sems = refs
    size = targets[0].shape[0]

    @pl.when(where_ref[0] == 0)
    def _():
        split_rows(where_ref, own, beside, size, held, sems, targets)

    @pl.when(where_ref[0] != 0)
    def _():
        count, step = gathered[0].shape[:2]
        copies = [pltpu.make_async_copy(ref, parts.at[i], part_sems.at[i]) for i, ref in enumerate(gathered)]
        start(copies)
        for i, copy in enumerate(copies):
            copy.wait()
            place = where_ref[1] if i < 2 else 1 - where_ref[1]
            for j in range(count):
                rows = pl.ds(pl.multiple_of(order_ref[i % 2 * count + j] * step, step), step)
                store_columns(targets, place, rows, parts[i, j])


def split_below(where, order, own, beside, gathered, after):
    hours, width = own.shape
    half = hours // 2
    return pl.pallas_call(
        functools.partial(below_kernel, len(after)),
        in_specs=[pl.BlockSpec(memory_space=pltpu.SMEM)] * 2 + anywhere(6 + len(after)),
        out_specs=in_vmem(2),
        out_shape=[jax.ShapeDtypeStruct((half, 2 * width), jnp.bfloat16)] * 2,
        scratch_shapes=split_scratch(half, width)
        + [pltpu.VMEM((4, *gathered[0].shape), jnp.float32), pltpu.SemaphoreType.DMA((4,))],
        compiler_params=pltpu.CompilerParams(vmem_limit_bytes=VMEM_LIMIT),
        cost_estimate=LIGHT,
        name="split_below",
    )(where, order, own, beside, *gathered, *after)


def filter_kernel(first_col, cols, space_count, where_ref, left, centre, right, kappa_left, kappa, kappa_right, *refs):
    mine_ref, other_ref, wide, once, scale = refs[-5:]
    rows, width, lanes = centre.shape
    around = width + 2 * EDGE
    core, space = where_ref[1], where_ref[2]
    zero = jnp.zeros((around, lanes), jnp.float32)
    for ref in (wide, once):
        ref[0] = zero
        ref[rows + 1] = zero
    wide[1 : rows + 1, EDGE - left.shape[1] : EDGE, :] = left[...]
    wide[1 : rows + 1, EDGE : EDGE + width, :] = centre[...]
    wide[1 : rows + 1, EDGE + width : EDGE + width + right.shape[1], :] = right[...]

    @pl.when(pl.program_id(0) == 0)
    def _():
        weights = jnp.concatenate([kappa_left[...].T[-EDGE:], kappa[...].T, kappa_right[...].T[:EDGE]], axis=0) + 4.0
        weights = weights[first_col : first_col + around]
        for row in range(rows):
            scale[row] = jnp.broadcast_to(weights[:, row : row + 1], scale.shape[1:])

    strip = scale.shape[2]
    column = space * cols + first_col - EDGE + lax.broadcasted_iota(jnp.int32, (around, strip), 0)
    inside = (column >= 0) & (column < space_count * cols)

    def operate(source, row, at):
        x = source[row + 1, :, at]
        beside = source[row, :, at] + source[row + 2, :, at] + pltpu.roll(x, 1, 0) + pltpu.roll(x, around - 1, 0)
        return scale[row] * x - beside

    for place in range(lanes // strip):
        at = slice(place * strip, (place + 1) * strip)

        def first(row, carry):
            value = operate(wide, row, at)
            if first_col == 0 or first_col + width == cols:
                value = jnp.where(inside, value, 0.0)
            once[row + 1, :, at] = value
            return carry

        def second(row, carry):
            mine_ref[row, :, at] = operate(once, row + core * (rows // 2), at)[EDGE : EDGE + width]
            other_ref[row, :, at] = operate(once, row + (1 - core) * (rows // 2), at)[EDGE : EDGE + width]
            return carry

        lax.fori_loop(0, rows, first, 0, unroll=4)
        lax.fori_loop(0, rows // 2, second, 0, unroll=2)


def filtered(where, latent, halos, kappa_sq, start, width, space_count, after):
    rows, cols, hours = latent.shape
    lanes = min(2 * LANES, hours)
    last = start + width

    def spec(columns, index):
        return pl.BlockSpec((rows, columns, lanes), lambda i, w: (0, index, i))

    low, high = halos
    left = (low, spec(low.shape[1], 0)) if start == 0 else (latent, spec(EDGE, start // EDGE - 1))
    centre = (latent, spec(width, start // width))
    right = (high, spec(high.shape[1], 0)) if last == cols else (latent, spec(EDGE, last // EDGE))
    fields, specs = zip(left, centre, right)
    kappa_specs = [
        pl.BlockSpec((rows, cols), lambda i, w, step=step: (0, jnp.clip(w[2] + step, 0, space_count - 1)))
        for step in (-1, 0, 1)
    ]
    half = rows // 2
    return pl.pallas_call(
        functools.partial(filter_kernel, start, cols, space_count),
        grid_spec=pltpu.PrefetchScalarGridSpec(
            num_scalar_prefetch=1,
            grid=(hours // lanes,),
            in_specs=[*specs, *kappa_specs] + anywhere(len(after)),
            out_specs=[pl.BlockSpec((half, width, lanes), lambda i, w: (0, 0, i))] * 2,
            scratch_shapes=[pltpu.VMEM((rows + 2, width + 2 * EDGE, lanes), jnp.float32)] * 2
            + [pltpu.VMEM((rows, width + 2 * EDGE, min(LANES, hours)), jnp.float32)],
        ),
        out_shape=[jax.ShapeDtypeStruct((half, width, hours), jnp.float32)] * 2,
        compiler_params=pltpu.CompilerParams(vmem_limit_bytes=VMEM_LIMIT),
        cost_estimate=LIGHT,
        name="filter",
    )(where, *fields, *[kappa_sq] * 3, *after)


def multiply(parts, weights, contract):
    (x_high, x_low), (w_high, w_low) = parts, weights
    dot = functools.partial(
        lax.dot_general,
        dimension_numbers=(((1,), (contract,)), ((), ())),
        preferred_element_type=jnp.float32,
    )
    return dot(x_high, w_high) + (dot(x_low, w_high) + dot(x_high, w_low))


def cut(refs, rows, columns):
    return tuple(ref[rows, columns] for ref in refs)


def blocks(size):
    step = min(FACTOR_BLOCK, size // 2)
    return [slice(i, i + step) for i in range(0, size, step)]


def place_series(source, parts):
    hours = source.shape[2]
    for place in range(2):
        for ref, value in zip(parts, split_bf16(source[place])):
            ref[:, place * hours : (place + 1) * hours] = value


def hours_of(at, size):
    place = at.start // (size // 2)
    return place, slice(at.start - place * size // 2, at.stop - place * size // 2)


def load(weights, buffer, sems):
    return [pltpu.make_async_copy(ref, buffer.at[part], sems.at[part]) for part, ref in enumerate(weights)]


def weight_scratch(size):
    return [pltpu.VMEM((2, size, size), jnp.bfloat16)], [pltpu.SemaphoreType.DMA((2,))]


def begin_kernel(tokens, where_ref, mine, across, *refs):
    refs = refs[tokens:]
    weights, sent, sums, fields, series, middle, held, diagonal, sems, weight_sems = refs[:2], *refs[2:]
    size = held.shape[1]
    core = where_ref[1]
    everything = slice(None)
    series, middle = [series.at[i] for i in range(2)], [middle.at[i] for i in range(2)]
    lower = where_ref[0] == 0
    upper = jnp.logical_not(lower)
    inputs = [
        pltpu.make_async_copy(mine, fields.at[core], sems.at[0]),
        pltpu.make_async_copy(across, fields.at[1 - core], sems.at[1]),
    ]
    hours = size // 2
    forward = [
        pltpu.make_async_copy(fields.at[i], sent.at[:, i * hours : (i + 1) * hours], sems.at[2 + i]) for i in range(2)
    ]
    loads = load(weights, diagonal, weight_sems)
    diagonal = [diagonal.at[i] for i in range(2)]
    start(inputs)
    start(loads)
    wait(inputs)

    @pl.when(upper)
    def _():
        start(forward)

    place_series(fields, series)
    wait(loads)
    for at in blocks(size):
        rows = slice(at.start, size)
        held[:, at] = multiply(cut(series, everything, rows), cut(diagonal, rows, at), 0)

    @pl.when(lower)
    def _():
        output = pltpu.make_async_copy(held, sent, sems.at[4])
        output.start()
        output.wait()

    @pl.when(upper)
    def _():
        for ref, part in zip(middle, split_bf16(held[...])):
            ref[...] = part
        for at in blocks(size):
            columns = slice(0, at.stop)
            held[:, at] = multiply(cut(middle, everything, columns), cut(diagonal, at, columns), 1)
        output = pltpu.make_async_copy(held, sums, sems.at[4])
        output.start()
        wait(forward)
        output.wait()


def begin(where, mine, across, diagonal, after):
    cells, hours = mine.shape
    size = 2 * hours
    operands = [mine, across, *after]
    return pl.pallas_call(
        functools.partial(begin_kernel, len(after)),
        in_specs=[pl.BlockSpec(memory_space=pltpu.SMEM)] + anywhere(len(operands) + 2),
        out_specs=anywhere(2),
        out_shape=[jax.ShapeDtypeStruct((cells, size), jnp.float32)] * 2,
        scratch_shapes=[
            pltpu.VMEM((2, cells, hours), jnp.float32),
            pltpu.VMEM((2, cells, size), jnp.bfloat16),
            pltpu.VMEM((2, cells, size), jnp.bfloat16),
            pltpu.VMEM((cells, size), jnp.float32),
            *weight_scratch(size)[0],
            pltpu.SemaphoreType.DMA((5,)),
            *weight_scratch(size)[1],
        ],
        compiler_params=pltpu.CompilerParams(vmem_limit_bytes=VMEM_LIMIT),
        cost_estimate=LIGHT,
        name="begin",
    )(where, *operands, *diagonal)


def send_hours(core, place, results, targets, sem):
    for target, chosen in zip(targets, (core == place, core != place)):

        @pl.when(chosen)
        def _():
            pltpu.make_async_copy(results.at[place], target, sem).start()


def wait_hours(core, results, targets, sems):
    for place in range(2):
        for target, chosen in zip(targets, (core == place, core != place)):

            @pl.when(chosen)
            def _():
                pltpu.make_async_copy(results.at[place], target, sems[place]).wait()


def end_kernel(tokens, where_ref, sent, sums, arrived, *refs):
    refs = refs[tokens:]
    diagonal_parts, below_parts, targets, refs = refs[:2], refs[2:4], refs[4:6], refs[6:]
    factors, terms, held, series, middle, results, diagonal, below, sems, diagonal_sems, below_sems = refs
    size = factors.shape[1]
    core = where_ref[1]
    everything = slice(None)
    series, middle = [series.at[i] for i in range(2)], [middle.at[i] for i in range(2)]
    lower = where_ref[0] == 0
    upper = jnp.logical_not(lower)

    def inputs(field, term):
        return [
            pltpu.make_async_copy(field, factors, sems.at[0]),
            pltpu.make_async_copy(term, terms, sems.at[1]),
        ]

    before = pltpu.make_async_copy(sums, held, sems.at[2])
    diagonal_loads = load(diagonal_parts, diagonal, diagonal_sems)
    halves = [slice(0, size // 2), slice(size // 2, size)]
    below_loads = [
        [
            pltpu.make_async_copy(ref.at[rows, :], below.at[part, rows, :], below_sems.at[part, i])
            for part, ref in enumerate(below_parts)
        ]
        for i, rows in enumerate(halves)
    ]
    diagonal, below = ([x.at[i] for i in range(2)] for x in (diagonal, below))

    @pl.when(lower)
    def _():
        start(inputs(arrived, sent))

    @pl.when(upper)
    def _():
        start(inputs(sent, arrived))

    for copies in below_loads:
        start(copies)

    @pl.when(lower)
    def _():
        start(diagonal_loads)

    @pl.when(upper)
    def _():
        before.start()

    @pl.when(lower)
    def _():
        wait(inputs(arrived, sent))

    @pl.when(upper)
    def _():
        wait(inputs(sent, arrived))

    for ref, part in zip(series, split_bf16(factors[...])):
        ref[...] = part
    for rows, copies in zip(halves, below_loads):
        wait(copies)
        for at in blocks(size):
            value = terms[:, at] + multiply(cut(series, everything, rows), cut(below, rows, at), 0)
            if rows.stop < size:
                terms[:, at] = value
            else:
                for ref, part in zip(middle, split_bf16(value)):
                    ref[:, at] = part

    @pl.when(lower)
    def _():
        wait(diagonal_loads)

    @pl.when(upper)
    def _():
        before.wait()

    for at in blocks(size):
        columns = slice(0, at.stop)
        place, piece = hours_of(at, size)

        @pl.when(lower)
        def _():
            results[place, :, piece] = multiply(cut(middle, everything, columns), cut(diagonal, at, columns), 1)

        @pl.when(upper)
        def _():
            value = multiply(cut(middle, everything, everything), cut(below, at, everything), 1)
            results[place, :, piece] = held[:, at] + value

        if at.stop == (place + 1) * size // 2:
            send_hours(core, place, results, targets, sems.at[3 + place])
    wait_hours(core, results, targets, [sems.at[3], sems.at[4]])


def end(where, sent, sums, arrived, diagonal, below, after):
    cells, size = sent.shape
    hours = size // 2
    operands = [sent, sums, arrived, *after]
    return pl.pallas_call(
        functools.partial(end_kernel, len(after)),
        in_specs=[pl.BlockSpec(memory_space=pltpu.SMEM)] + anywhere(len(operands) + 4),
        out_specs=anywhere(2),
        out_shape=[jax.ShapeDtypeStruct((cells, hours), jnp.float32)] * 2,
        scratch_shapes=[pltpu.VMEM((cells, size), jnp.float32)] * 3
        + [pltpu.VMEM((2, cells, size), jnp.bfloat16)] * 2
        + [pltpu.VMEM((2, cells, hours), jnp.float32)]
        + weight_scratch(size)[0] * 2
        + [pltpu.SemaphoreType.DMA((5,)), pltpu.SemaphoreType.DMA((2,)), pltpu.SemaphoreType.DMA((2, 2))],
        compiler_params=pltpu.CompilerParams(vmem_limit_bytes=VMEM_LIMIT),
        cost_estimate=LIGHT,
        name="end",
    )(where, *operands, *diagonal, *below)


def join_kernel(count, *refs):
    out, held, sems = refs[-3:]
    first = 0
    group = []
    for i, ref in enumerate(refs[:count]):
        group.append(pltpu.make_async_copy(ref, held.at[pl.ds(first, ref.shape[0])], sems.at[i]))
        first += ref.shape[0]
    start(group)
    wait(group)
    output = pltpu.make_async_copy(held, out, sems.at[count])
    output.start()
    output.wait()


def join(pieces, after):
    shape = (sum(x.shape[0] for x in pieces), *pieces[0].shape[1:])
    return pl.pallas_call(
        functools.partial(join_kernel, len(pieces)),
        in_specs=anywhere(len(pieces) + len(after)),
        out_specs=pl.BlockSpec(memory_space=pl.ANY),
        out_shape=jax.ShapeDtypeStruct(shape, pieces[0].dtype),
        scratch_shapes=[pltpu.VMEM(shape, pieces[0].dtype), pltpu.SemaphoreType.DMA((len(pieces) + 1,))],
        compiler_params=pltpu.CompilerParams(vmem_limit_bytes=VMEM_LIMIT),
        cost_estimate=LIGHT,
        name="join",
    )(*pieces, *after)


def finish_kernel(turns, where_ref, step_ref, own, beside, latent_ref, events_ref, base_ref, draw_ref, *refs):
    gradient_ref, proposal_ref = refs[-2:]
    latent = latent_ref[...]
    spread = jnp.sqrt(jnp.full((1, 1, latent.shape[2]), 2.0 * step_ref[0]))
    data = events_ref[...].astype(jnp.float32) - jnp.exp(base_ref[...] + latent)
    for i, turn in enumerate(turns):
        prior = (own, beside)[turn]

        @pl.when(pl.program_id(0) == i)
        def _():
            slope = data - prior[...]
            gradient_ref[...] = slope
            proposal_ref[...] = latent + step_ref[0] * slope + spread * draw_ref[...]


def finish(where, steps, priors, fields, start, width, outs, after, turns):
    rows, cols, hours = fields[0].shape
    half = rows // 2
    shape = (half, width, hours)
    held = [prior.reshape(shape) for prior in priors]
    held_spec = pl.BlockSpec(shape, lambda i, w, s: (0, 0, 0))
    field_spec = pl.BlockSpec(shape, lambda i, w, s: ((w[1] + i + turns[0]) % 2, start // width, 0))
    out = jax.ShapeDtypeStruct((rows, cols, hours), jnp.float32)
    return pl.pallas_call(
        functools.partial(finish_kernel, turns),
        grid_spec=pltpu.PrefetchScalarGridSpec(
            num_scalar_prefetch=2,
            grid=(len(turns),),
            in_specs=[held_spec] * 2 + [field_spec] * 4 + anywhere(len(outs) + len(after)),
            out_specs=[field_spec] * 2,
        ),
        out_shape=[out, out],
        input_output_aliases={8 + i: i for i in range(len(outs))},
        compiler_params=pltpu.CompilerParams(vmem_limit_bytes=VMEM_LIMIT),
        cost_estimate=LIGHT,
        name="finish",
    )(where, steps, *held, *fields, *outs, *after)


def local(latent, events, log_base, innovation, kappa_sq, chol_factor, step_size):
    rows, cols, hours = latent.shape
    place = lax.axis_index("tm")
    upper, core = place // 2, place % 2
    space = lax.axis_index("space")
    space_count = lax.axis_size("space")
    where = jnp.stack([upper, core, space]).astype(jnp.int32)

    def beside(x):
        return lax.ppermute(x, "tm", [(0, 1), (1, 0), (2, 3), (3, 2)])

    def exchange(x):
        return lax.ppermute(x, "tm", [(0, 2), (1, 3), (2, 0), (3, 1)])

    across_core = beside(chol_factor)
    forward = [(i, i + 1) for i in range(space_count - 1)]
    backward = [(i + 1, i) for i in range(space_count - 1)]
    halos = (
        lax.ppermute(latent[:, cols - 2 :], "space", forward),
        lax.ppermute(latent[:, :2], "space", backward),
    )
    fields = (latent, events, log_base, innovation)
    mine, others, sent, sums, arrived, totals = ({} for _ in range(6))

    share = 2 * hours // space_count
    slab = lax.dynamic_slice(chol_factor, (2 * hours + space * share, jnp.int32(0)), (share, hours))
    held = lax.ppermute(slab, "tm", [(0, 2), (1, 3)])[None]
    order = [0]

    def double(x):
        bit = space_count // 2 // len(order)
        order.extend([i ^ bit for i in order])
        return lax.ppermute(x, "space", [(i, i ^ bit) for i in range(space_count)])

    received = double(held)
    transfers = {"slab": [held], "halo": [*halos]}
    token, outs = [], []
    for name in ORDER:
        kind, k = name[0], int(name[1:] or 0)
        after = token + [x for pin in PINS.get(name, ()) for x in transfers[pin]]
        if kind == "F":
            made = filtered(where, latent, halos, kappa_sq, *CHUNKS[k], space_count, after)
            mine[k], away = (x.reshape(-1, hours) for x in made)
            others[k] = beside(away)
            token = [mine[k]]
        elif kind == "D":
            diagonal = split_diagonal(where, chol_factor, across_core, after)
            token = [diagonal[0]]
        elif kind == "B":
            sent[k], sums[k] = begin(where, mine[k], others[k], diagonal, after)
            arrived[k] = exchange(sent[k])
            transfers["Y" + name[1:]] = [arrived[k]]
            token = [sent[k]]
        elif kind == "J" and k < 3:
            held = join([held, received], after)
            received = double(held)
            token = [held]
        elif kind == "J":
            received = join([received], after)
            token = [received]
        elif kind == "S":
            gathered = [held, received, beside(held), beside(received)]
            order = space.astype(jnp.int32) ^ jnp.array(order, jnp.int32)
            below = split_below(where, order, chol_factor, across_core, gathered, after)
            token = [below[0]]
        elif kind == "E":
            own, across = end(where, sent[k], sums[k], arrived[k], diagonal, below, after)
            totals[k] = own, beside(across)
            token = [own]
        else:
            own, across = totals[k]
            turns = {"f": (0, 1), "g": (0,), "h": (1,)}[kind]
            priors = (own, own) if kind == "g" else (own, across)
            after = [x for x in after if not any(x is y for y in outs)]
            outs = finish(where, step_size, priors, fields, *CHUNKS[k], outs, after, turns)
            token = [outs[0]]
    return outs


def plain(latent, events, log_base, innovation, kappa_sq, chol_factor, step_size):
    rows, cols, hours = latent.shape
    space = lax.axis_index("space")
    count = lax.axis_size("space")
    forward = [(i, i + 1) for i in range(count - 1)]
    backward = [(i + 1, i) for i in range(count - 1)]
    kappa = lax.dynamic_slice(kappa_sq, (jnp.int32(0), space * cols), (rows, cols))

    def operate(field):
        low = lax.ppermute(field[:, -1:], "space", forward)
        high = lax.ppermute(field[:, :1], "space", backward)
        row_padded = jnp.pad(field, ((1, 1), (0, 0), (0, 0)))
        wide = jnp.concatenate([low, field, high], axis=1)
        beside = row_padded[2:] + row_padded[:-2] + wide[:, 2:] + wide[:, :-2]
        return (kappa[:, :, None] + 4.0) * field - beside

    dot = functools.partial(lax.dot_general, precision=lax.Precision.HIGHEST, preferred_element_type=jnp.float32)
    series = operate(operate(latent)).reshape(rows * cols, hours)
    projected = dot(lax.all_gather(series, "tm", axis=1, tiled=True), chol_factor, (((1,), (0,)), ((), ())))
    sums = dot(chol_factor, projected, (((1,), (1,)), ((), ())))
    by_hour = lax.psum_scatter(sums, "tm", scatter_dimension=0, tiled=True)
    prior = by_hour.T.reshape(rows, cols, hours)
    gradient = events.astype(jnp.float32) - jnp.exp(log_base + latent) - prior
    proposal = latent + step_size[0] * gradient + jnp.sqrt(2.0 * step_size[0]) * innovation
    return gradient, proposal


def solution(mesh):
    in_specs = (
        P(None, "space", "tm"),
        P(None, "space", "tm"),
        P(None, "space", "tm"),
        P(None, "space", "tm"),
        P(),
        P(None, "tm"),
        P(),
    )
    out_specs = (P(None, "space", "tm"), P(None, "space", "tm"))
    body = local if mesh.shape["tm"] == 4 and mesh.shape["space"] == 8 else plain
    return jax.shard_map(body, mesh=mesh, in_specs=in_specs, out_specs=out_specs, check_vma=False)
```

```python
import functools

import jax
import jax.numpy as jnp
from jax import lax
from jax.experimental import pallas as pl
from jax.experimental.pallas import tpu as pltpu
from jax.sharding import PartitionSpec as P

EDGE = 8
LANES = 128
CHUNKS = ((32, 32), (64, 32), (0, 32), (96, 32))
ORDER = ("F0", "B0", "F1", "B1", "J1", "F2", "J2", "B2", "F3", "B3", "J3", "S", "E0", "E1", "E2", "f0", "f1", "f2", "E3", "f3")
PINS = {"F1": ("slab",), "F2": ("halo",), "J2": ("Y0",), "J3": ("Y1",)}
FACTOR_BLOCK = 256
VMEM_LIMIT = 63 * 1024 * 1024
LIGHT = pl.CostEstimate(flops=0, bytes_accessed=4096, transcendentals=0)


def split_bf16(x):
    high = x.astype(jnp.bfloat16)
    return high, (x - high.astype(jnp.float32)).astype(jnp.bfloat16)


def anywhere(count):
    return [pl.BlockSpec(memory_space=pl.ANY)] * count


def in_vmem(count):
    return [pl.BlockSpec(memory_space=pltpu.VMEM)] * count


def start(group):
    for copy in group:
        copy.start()


def wait(group):
    for copy in group:
        copy.wait()


def split_rows(where_ref, own, beside, first, held, sems, targets):
    size, width = targets[0].shape[0], own.shape[1]
    step = held.shape[2]
    places = (where_ref[1], 1 - where_ref[1])
    groups = [
        [
            pltpu.make_async_copy(source.at[pl.ds(first + row, step)], held.at[i, j], sems.at[i, j])
            for j, source in enumerate((own, beside))
        ]
        for i, row in enumerate(range(0, size, step))
    ]
    for copies in groups:
        start(copies)
    for i, copies in enumerate(groups):
        wait(copies)
        for j, place in enumerate(places):
            store_columns(targets, place, slice(i * step, (i + 1) * step), held[i, j])


def store_columns(targets, place, rows, values):
    width = values.shape[1]
    at = pl.ds(pl.multiple_of(place * width, width), width)
    for ref, value in zip(targets, split_bf16(values)):
        ref[rows, at] = value


def split_scratch(size, width):
    step = min(FACTOR_BLOCK, size)
    return [pltpu.VMEM((size // step, 2, step, width), jnp.float32), pltpu.SemaphoreType.DMA((size // step, 2))]


def below_kernel(tokens, where_ref, order_ref, own, beside, *refs):
    gathered, refs = refs[:4], refs[4 + tokens :]
    *targets, held, sems, parts, part_sems = refs
    size = targets[0].shape[0]

    @pl.when(where_ref[0] == 0)
    def _():
        split_rows(where_ref, own, beside, size, held, sems, targets)

    @pl.when(where_ref[0] != 0)
    def _():
        count, step = gathered[0].shape[:2]
        copies = [pltpu.make_async_copy(ref, parts.at[i], part_sems.at[i]) for i, ref in enumerate(gathered)]
        start(copies)
        for i, copy in enumerate(copies):
            copy.wait()
            place = where_ref[1] if i < 2 else 1 - where_ref[1]
            for j in range(count):
                rows = pl.ds(pl.multiple_of(order_ref[i % 2 * count + j] * step, step), step)
                store_columns(targets, place, rows, parts[i, j])


def split_below(where, order, own, beside, gathered, after):
    hours, width = own.shape
    half = hours // 2
    return pl.pallas_call(
        functools.partial(below_kernel, len(after)),
        in_specs=[pl.BlockSpec(memory_space=pltpu.SMEM)] * 2 + anywhere(6 + len(after)),
        out_specs=in_vmem(2),
        out_shape=[jax.ShapeDtypeStruct((half, 2 * width), jnp.bfloat16)] * 2,
        scratch_shapes=split_scratch(half, width)
        + [pltpu.VMEM((4, *gathered[0].shape), jnp.float32), pltpu.SemaphoreType.DMA((4,))],
        compiler_params=pltpu.CompilerParams(vmem_limit_bytes=VMEM_LIMIT),
        cost_estimate=LIGHT,
        name="split_below",
    )(where, order, own, beside, *gathered, *after)


def filter_kernel(first_col, cols, space_count, where_ref, left, centre, right, kappa_left, kappa, kappa_right, *refs):
    mine_ref, other_ref, wide, once, scale = refs[-5:]
    rows, width, lanes = centre.shape
    around = width + 2 * EDGE
    core, space = where_ref[1], where_ref[2]
    zero = jnp.zeros((around, lanes), jnp.float32)
    for ref in (wide, once):
        ref[0] = zero
        ref[rows + 1] = zero
    wide[1 : rows + 1, EDGE - left.shape[1] : EDGE, :] = left[...]
    wide[1 : rows + 1, EDGE : EDGE + width, :] = centre[...]
    wide[1 : rows + 1, EDGE + width : EDGE + width + right.shape[1], :] = right[...]

    @pl.when(pl.program_id(0) == 0)
    def _():
        weights = jnp.concatenate([kappa_left[...].T[-EDGE:], kappa[...].T, kappa_right[...].T[:EDGE]], axis=0) + 4.0
        weights = weights[first_col : first_col + around]
        for row in range(rows):
            scale[row] = jnp.broadcast_to(weights[:, row : row + 1], scale.shape[1:])

    strip = scale.shape[2]
    column = space * cols + first_col - EDGE + lax.broadcasted_iota(jnp.int32, (around, strip), 0)
    inside = (column >= 0) & (column < space_count * cols)

    def operate(source, row, at):
        x = source[row + 1, :, at]
        beside = source[row, :, at] + source[row + 2, :, at] + pltpu.roll(x, 1, 0) + pltpu.roll(x, around - 1, 0)
        return scale[row] * x - beside

    for place in range(lanes // strip):
        at = slice(place * strip, (place + 1) * strip)

        def first(row, carry):
            value = operate(wide, row, at)
            if first_col == 0 or first_col + width == cols:
                value = jnp.where(inside, value, 0.0)
            once[row + 1, :, at] = value
            return carry

        def second(row, carry):
            mine_ref[row, :, at] = operate(once, row + core * (rows // 2), at)[EDGE : EDGE + width]
            other_ref[row, :, at] = operate(once, row + (1 - core) * (rows // 2), at)[EDGE : EDGE + width]
            return carry

        lax.fori_loop(0, rows, first, 0, unroll=4)
        lax.fori_loop(0, rows // 2, second, 0, unroll=2)


def filtered(where, latent, halos, kappa_sq, start, width, space_count, after):
    rows, cols, hours = latent.shape
    lanes = min(2 * LANES, hours)
    last = start + width

    def spec(columns, index):
        return pl.BlockSpec((rows, columns, lanes), lambda i, w: (0, index, i))

    low, high = halos
    left = (low, spec(low.shape[1], 0)) if start == 0 else (latent, spec(EDGE, start // EDGE - 1))
    centre = (latent, spec(width, start // width))
    right = (high, spec(high.shape[1], 0)) if last == cols else (latent, spec(EDGE, last // EDGE))
    fields, specs = zip(left, centre, right)
    kappa_specs = [
        pl.BlockSpec((rows, cols), lambda i, w, step=step: (0, jnp.clip(w[2] + step, 0, space_count - 1)))
        for step in (-1, 0, 1)
    ]
    half = rows // 2
    return pl.pallas_call(
        functools.partial(filter_kernel, start, cols, space_count),
        grid_spec=pltpu.PrefetchScalarGridSpec(
            num_scalar_prefetch=1,
            grid=(hours // lanes,),
            in_specs=[*specs, *kappa_specs] + anywhere(len(after)),
            out_specs=[pl.BlockSpec((half, width, lanes), lambda i, w: (0, 0, i))] * 2,
            scratch_shapes=[pltpu.VMEM((rows + 2, width + 2 * EDGE, lanes), jnp.float32)] * 2
            + [pltpu.VMEM((rows, width + 2 * EDGE, min(LANES, hours)), jnp.float32)],
        ),
        out_shape=[jax.ShapeDtypeStruct((half, width, hours), jnp.float32)] * 2,
        compiler_params=pltpu.CompilerParams(vmem_limit_bytes=VMEM_LIMIT),
        cost_estimate=LIGHT,
        name="filter",
    )(where, *fields, *[kappa_sq] * 3, *after)


def multiply(parts, weights, contract):
    (x_high, x_low), (w_high, w_low) = parts, weights
    dot = functools.partial(
        lax.dot_general,
        dimension_numbers=(((1,), (contract,)), ((), ())),
        preferred_element_type=jnp.float32,
    )
    return dot(x_high, w_high) + (dot(x_low, w_high) + dot(x_high, w_low))


def cut(refs, rows, columns):
    return tuple(ref[rows, columns] for ref in refs)


def blocks(size):
    step = min(FACTOR_BLOCK, size // 2)
    return [slice(i, i + step) for i in range(0, size, step)]


def place_series(source, parts):
    hours = source.shape[2]
    for place in range(2):
        for ref, value in zip(parts, split_bf16(source[place])):
            ref[:, place * hours : (place + 1) * hours] = value


def hours_of(at, size):
    place = at.start // (size // 2)
    return place, slice(at.start - place * size // 2, at.stop - place * size // 2)


def load(weights, buffer, sems):
    return [pltpu.make_async_copy(ref, buffer.at[part], sems.at[part]) for part, ref in enumerate(weights)]


def weight_scratch(size):
    return [pltpu.VMEM((2, size, size), jnp.bfloat16)], [pltpu.SemaphoreType.DMA((2,))]


def begin_kernel(tokens, first, where_ref, mine, across, *refs):
    refs = refs[tokens:]
    if first:
        own, beside, sent, sums, *parts = refs[:6]
        fields, series, middle, held, diagonal, sems, part_sems, rows_held, rows_sems = refs[6:]
    else:
        weights, sent, sums = refs[:2], *refs[2:4]
        fields, series, middle, held, diagonal, sems, weight_sems = refs[4:]
    size = held.shape[1]
    core = where_ref[1]
    everything = slice(None)
    series, middle = [series.at[i] for i in range(2)], [middle.at[i] for i in range(2)]
    lower = where_ref[0] == 0
    upper = jnp.logical_not(lower)
    inputs = [
        pltpu.make_async_copy(mine, fields.at[core], sems.at[0]),
        pltpu.make_async_copy(across, fields.at[1 - core], sems.at[1]),
    ]
    hours = size // 2
    forward = [
        pltpu.make_async_copy(fields.at[i], sent.at[:, i * hours : (i + 1) * hours], sems.at[2 + i]) for i in range(2)
    ]
    start(inputs)
    if first:
        stores = [pltpu.make_async_copy(diagonal.at[i], part, part_sems.at[i]) for i, part in enumerate(parts)]
        diagonal = [diagonal.at[i] for i in range(2)]
        split_rows(where_ref, own, beside, where_ref[0] * size, rows_held, rows_sems, diagonal)
        start(stores)
    else:
        loads = load(weights, diagonal, weight_sems)
        diagonal = [diagonal.at[i] for i in range(2)]
        start(loads)
    wait(inputs)

    @pl.when(upper)
    def _():
        start(forward)

    place_series(fields, series)
    if not first:
        wait(loads)
    for at in blocks(size):
        rows = slice(at.start, size)
        held[:, at] = multiply(cut(series, everything, rows), cut(diagonal, rows, at), 0)

    @pl.when(lower)
    def _():
        output = pltpu.make_async_copy(held, sent, sems.at[4])
        output.start()
        output.wait()

    @pl.when(upper)
    def _():
        for ref, part in zip(middle, split_bf16(held[...])):
            ref[...] = part
        for at in blocks(size):
            columns = slice(0, at.stop)
            held[:, at] = multiply(cut(middle, everything, columns), cut(diagonal, at, columns), 1)
        output = pltpu.make_async_copy(held, sums, sems.at[4])
        output.start()
        wait(forward)
        output.wait()

    if first:
        wait(stores)


def begin(where, mine, across, diagonal, after, columns=None):
    cells, hours = mine.shape
    size = 2 * hours
    operands = [mine, across, *after, *(columns or diagonal)]
    first = columns is not None
    outs = [jax.ShapeDtypeStruct((cells, size), jnp.float32)] * 2
    buffers, sems = weight_scratch(size)
    scratch = [
        pltpu.VMEM((2, cells, hours), jnp.float32),
        pltpu.VMEM((2, cells, size), jnp.bfloat16),
        pltpu.VMEM((2, cells, size), jnp.bfloat16),
        pltpu.VMEM((cells, size), jnp.float32),
        *buffers,
        pltpu.SemaphoreType.DMA((5,)),
        *sems,
    ]
    if first:
        outs = outs + [jax.ShapeDtypeStruct((size, size), jnp.bfloat16)] * 2
        scratch = scratch + split_scratch(size, hours)
    return pl.pallas_call(
        functools.partial(begin_kernel, len(after), first),
        in_specs=[pl.BlockSpec(memory_space=pltpu.SMEM)] + anywhere(len(operands)),
        out_specs=anywhere(len(outs)),
        out_shape=outs,
        scratch_shapes=scratch,
        compiler_params=pltpu.CompilerParams(vmem_limit_bytes=VMEM_LIMIT),
        cost_estimate=LIGHT,
        name="begin",
    )(where, *operands)


def send_hours(core, place, results, targets, sem):
    for target, chosen in zip(targets, (core == place, core != place)):

        @pl.when(chosen)
        def _():
            pltpu.make_async_copy(results.at[place], target, sem).start()


def wait_hours(core, results, targets, sems):
    for place in range(2):
        for target, chosen in zip(targets, (core == place, core != place)):

            @pl.when(chosen)
            def _():
                pltpu.make_async_copy(results.at[place], target, sems[place]).wait()


def end_kernel(tokens, where_ref, sent, sums, arrived, *refs):
    refs = refs[tokens:]
    diagonal_parts, below_parts, targets, refs = refs[:2], refs[2:4], refs[4:6], refs[6:]
    factors, terms, held, series, middle, results, diagonal, below, sems, diagonal_sems, below_sems = refs
    size = factors.shape[1]
    core = where_ref[1]
    everything = slice(None)
    series, middle = [series.at[i] for i in range(2)], [middle.at[i] for i in range(2)]
    lower = where_ref[0] == 0
    upper = jnp.logical_not(lower)

    def inputs(field, term):
        return [
            pltpu.make_async_copy(field, factors, sems.at[0]),
            pltpu.make_async_copy(term, terms, sems.at[1]),
        ]

    before = pltpu.make_async_copy(sums, held, sems.at[2])
    diagonal_loads = load(diagonal_parts, diagonal, diagonal_sems)
    halves = [slice(0, size // 2), slice(size // 2, size)]
    below_loads = [
        [
            pltpu.make_async_copy(ref.at[rows, :], below.at[part, rows, :], below_sems.at[part, i])
            for part, ref in enumerate(below_parts)
        ]
        for i, rows in enumerate(halves)
    ]
    diagonal, below = ([x.at[i] for i in range(2)] for x in (diagonal, below))

    @pl.when(lower)
    def _():
        start(inputs(arrived, sent))

    @pl.when(upper)
    def _():
        start(inputs(sent, arrived))

    for copies in below_loads:
        start(copies)

    @pl.when(lower)
    def _():
        start(diagonal_loads)

    @pl.when(upper)
    def _():
        before.start()

    @pl.when(lower)
    def _():
        wait(inputs(arrived, sent))

    @pl.when(upper)
    def _():
        wait(inputs(sent, arrived))

    for ref, part in zip(series, split_bf16(factors[...])):
        ref[...] = part
    for rows, copies in zip(halves, below_loads):
        wait(copies)
        for at in blocks(size):
            value = terms[:, at] + multiply(cut(series, everything, rows), cut(below, rows, at), 0)
            if rows.stop < size:
                terms[:, at] = value
            else:
                for ref, part in zip(middle, split_bf16(value)):
                    ref[:, at] = part

    @pl.when(lower)
    def _():
        wait(diagonal_loads)

    @pl.when(upper)
    def _():
        before.wait()

    for at in blocks(size):
        columns = slice(0, at.stop)
        place, piece = hours_of(at, size)

        @pl.when(lower)
        def _():
            results[place, :, piece] = multiply(cut(middle, everything, columns), cut(diagonal, at, columns), 1)

        @pl.when(upper)
        def _():
            value = multiply(cut(middle, everything, everything), cut(below, at, everything), 1)
            results[place, :, piece] = held[:, at] + value

        if at.stop == (place + 1) * size // 2:
            send_hours(core, place, results, targets, sems.at[3 + place])
    wait_hours(core, results, targets, [sems.at[3], sems.at[4]])


def end(where, sent, sums, arrived, diagonal, below, after):
    cells, size = sent.shape
    hours = size // 2
    operands = [sent, sums, arrived, *after]
    return pl.pallas_call(
        functools.partial(end_kernel, len(after)),
        in_specs=[pl.BlockSpec(memory_space=pltpu.SMEM)] + anywhere(len(operands) + 4),
        out_specs=anywhere(2),
        out_shape=[jax.ShapeDtypeStruct((cells, hours), jnp.float32)] * 2,
        scratch_shapes=[pltpu.VMEM((cells, size), jnp.float32)] * 3
        + [pltpu.VMEM((2, cells, size), jnp.bfloat16)] * 2
        + [pltpu.VMEM((2, cells, hours), jnp.float32)]
        + weight_scratch(size)[0] * 2
        + [pltpu.SemaphoreType.DMA((5,)), pltpu.SemaphoreType.DMA((2,)), pltpu.SemaphoreType.DMA((2, 2))],
        compiler_params=pltpu.CompilerParams(vmem_limit_bytes=VMEM_LIMIT),
        cost_estimate=LIGHT,
        name="end",
    )(where, *operands, *diagonal, *below)


def join_kernel(count, *refs):
    out, held, sems = refs[-3:]
    first = 0
    group = []
    for i, ref in enumerate(refs[:count]):
        group.append(pltpu.make_async_copy(ref, held.at[pl.ds(first, ref.shape[0])], sems.at[i]))
        first += ref.shape[0]
    start(group)
    wait(group)
    output = pltpu.make_async_copy(held, out, sems.at[count])
    output.start()
    output.wait()


def join(pieces, after):
    shape = (sum(x.shape[0] for x in pieces), *pieces[0].shape[1:])
    return pl.pallas_call(
        functools.partial(join_kernel, len(pieces)),
        in_specs=anywhere(len(pieces) + len(after)),
        out_specs=pl.BlockSpec(memory_space=pl.ANY),
        out_shape=jax.ShapeDtypeStruct(shape, pieces[0].dtype),
        scratch_shapes=[pltpu.VMEM(shape, pieces[0].dtype), pltpu.SemaphoreType.DMA((len(pieces) + 1,))],
        compiler_params=pltpu.CompilerParams(vmem_limit_bytes=VMEM_LIMIT),
        cost_estimate=LIGHT,
        name="join",
    )(*pieces, *after)


def finish_kernel(turns, where_ref, step_ref, own, beside, latent_ref, events_ref, base_ref, draw_ref, *refs):
    gradient_ref, proposal_ref = refs[-2:]
    latent = latent_ref[...]
    spread = jnp.sqrt(jnp.full((1, 1, latent.shape[2]), 2.0 * step_ref[0]))
    data = events_ref[...].astype(jnp.float32) - jnp.exp(base_ref[...] + latent)
    for i, turn in enumerate(turns):
        prior = (own, beside)[turn]

        @pl.when(pl.program_id(0) == i)
        def _():
            slope = data - prior[...]
            gradient_ref[...] = slope
            proposal_ref[...] = latent + step_ref[0] * slope + spread * draw_ref[...]


def finish(where, steps, priors, fields, start, width, outs, after, turns):
    rows, cols, hours = fields[0].shape
    half = rows // 2
    shape = (half, width, hours)
    held = [prior.reshape(shape) for prior in priors]
    held_spec = pl.BlockSpec(shape, lambda i, w, s: (0, 0, 0))
    field_spec = pl.BlockSpec(shape, lambda i, w, s: ((w[1] + i + turns[0]) % 2, start // width, 0))
    out = jax.ShapeDtypeStruct((rows, cols, hours), jnp.float32)
    return pl.pallas_call(
        functools.partial(finish_kernel, turns),
        grid_spec=pltpu.PrefetchScalarGridSpec(
            num_scalar_prefetch=2,
            grid=(len(turns),),
            in_specs=[held_spec] * 2 + [field_spec] * 4 + anywhere(len(outs) + len(after)),
            out_specs=[field_spec] * 2,
        ),
        out_shape=[out, out],
        input_output_aliases={8 + i: i for i in range(len(outs))},
        compiler_params=pltpu.CompilerParams(vmem_limit_bytes=VMEM_LIMIT),
        cost_estimate=LIGHT,
        name="finish",
    )(where, steps, *held, *fields, *outs, *after)


def local(latent, events, log_base, innovation, kappa_sq, chol_factor, step_size):
    rows, cols, hours = latent.shape
    place = lax.axis_index("tm")
    upper, core = place // 2, place % 2
    space = lax.axis_index("space")
    space_count = lax.axis_size("space")
    where = jnp.stack([upper, core, space]).astype(jnp.int32)

    def beside(x):
        return lax.ppermute(x, "tm", [(0, 1), (1, 0), (2, 3), (3, 2)])

    def exchange(x):
        return lax.ppermute(x, "tm", [(0, 2), (1, 3), (2, 0), (3, 1)])

    across_core = beside(chol_factor)
    forward = [(i, i + 1) for i in range(space_count - 1)]
    backward = [(i + 1, i) for i in range(space_count - 1)]
    halos = (
        lax.ppermute(latent[:, cols - 2 :], "space", forward),
        lax.ppermute(latent[:, :2], "space", backward),
    )
    fields = (latent, events, log_base, innovation)
    mine, others, sent, sums, arrived, totals = ({} for _ in range(6))

    share = 2 * hours // space_count
    slab = lax.dynamic_slice(chol_factor, (2 * hours + space * share, jnp.int32(0)), (share, hours))
    held = lax.ppermute(slab, "tm", [(0, 2), (1, 3)])[None]
    order = [0]

    def double(x):
        bit = space_count // 2 // len(order)
        order.extend([i ^ bit for i in order])
        return lax.ppermute(x, "space", [(i, i ^ bit) for i in range(space_count)])

    received = double(held)
    transfers = {"slab": [held], "halo": [*halos]}
    token, outs, diagonal = [], [], []
    for name in ORDER:
        kind, k = name[0], int(name[1:] or 0)
        after = token + [x for pin in PINS.get(name, ()) for x in transfers[pin]]
        if kind == "F":
            made = filtered(where, latent, halos, kappa_sq, *CHUNKS[k], space_count, after)
            mine[k], away = (x.reshape(-1, hours) for x in made)
            others[k] = beside(away)
            token = [mine[k]]
        elif kind == "B":
            columns = None if diagonal else (chol_factor, across_core)
            sent[k], sums[k], *parts = begin(where, mine[k], others[k], diagonal, after, columns)
            diagonal = diagonal or parts
            arrived[k] = exchange(sent[k])
            transfers["Y" + name[1:]] = [arrived[k]]
            token = [sent[k]]
        elif kind == "J" and k < 3:
            held = join([held, received], after)
            received = double(held)
            token = [held]
        elif kind == "J":
            received = join([received], after)
            token = [received]
        elif kind == "S":
            gathered = [held, received, beside(held), beside(received)]
            order = space.astype(jnp.int32) ^ jnp.array(order, jnp.int32)
            below = split_below(where, order, chol_factor, across_core, gathered, after)
            token = [below[0]]
        elif kind == "E":
            own, across = end(where, sent[k], sums[k], arrived[k], diagonal, below, after)
            totals[k] = own, beside(across)
            token = [own]
        else:
            own, across = totals[k]
            turns = {"f": (0, 1), "g": (0,), "h": (1,)}[kind]
            priors = (own, own) if kind == "g" else (own, across)
            after = [x for x in after if not any(x is y for y in outs)]
            outs = finish(where, step_size, priors, fields, *CHUNKS[k], outs, after, turns)
            token = [outs[0]]
    return outs


def plain(latent, events, log_base, innovation, kappa_sq, chol_factor, step_size):
    rows, cols, hours = latent.shape
    space = lax.axis_index("space")
    count = lax.axis_size("space")
    forward = [(i, i + 1) for i in range(count - 1)]
    backward = [(i + 1, i) for i in range(count - 1)]
    kappa = lax.dynamic_slice(kappa_sq, (jnp.int32(0), space * cols), (rows, cols))

    def operate(field):
        low = lax.ppermute(field[:, -1:], "space", forward)
        high = lax.ppermute(field[:, :1], "space", backward)
        row_padded = jnp.pad(field, ((1, 1), (0, 0), (0, 0)))
        wide = jnp.concatenate([low, field, high], axis=1)
        beside = row_padded[2:] + row_padded[:-2] + wide[:, 2:] + wide[:, :-2]
        return (kappa[:, :, None] + 4.0) * field - beside

    dot = functools.partial(lax.dot_general, precision=lax.Precision.HIGHEST, preferred_element_type=jnp.float32)
    series = operate(operate(latent)).reshape(rows * cols, hours)
    projected = dot(lax.all_gather(series, "tm", axis=1, tiled=True), chol_factor, (((1,), (0,)), ((), ())))
    sums = dot(chol_factor, projected, (((1,), (1,)), ((), ())))
    by_hour = lax.psum_scatter(sums, "tm", scatter_dimension=0, tiled=True)
    prior = by_hour.T.reshape(rows, cols, hours)
    gradient = events.astype(jnp.float32) - jnp.exp(log_base + latent) - prior
    proposal = latent + step_size[0] * gradient + jnp.sqrt(2.0 * step_size[0]) * innovation
    return gradient, proposal


def solution(mesh):
    in_specs = (
        P(None, "space", "tm"),
        P(None, "space", "tm"),
        P(None, "space", "tm"),
        P(None, "space", "tm"),
        P(),
        P(None, "tm"),
        P(),
    )
    out_specs = (P(None, "space", "tm"), P(None, "space", "tm"))
    body = local if mesh.shape["tm"] == 4 and mesh.shape["space"] == 8 else plain
    return jax.shard_map(body, mesh=mesh, in_specs=in_specs, out_specs=out_specs, check_vma=False)
```

```python
import functools

import jax
import jax.numpy as jnp
from jax import lax
from jax.experimental import pallas as pl
from jax.experimental.pallas import tpu as pltpu
from jax.sharding import PartitionSpec as P

EDGE = 8
LANES = 128
CHUNKS = ((32, 32), (64, 32), (0, 32), (96, 32))
ORDER = ("F0", "B0", "F1", "B1", "J1", "F2", "J2", "B2", "F3", "B3", "J3", "S", "E0", "E1", "E2", "f0", "f1", "f2", "E3", "f3")
PINS = {"F1": ("slab",), "F2": ("halo",), "J2": ("Y0",), "J3": ("Y1",)}
FACTOR_BLOCK = 256
VMEM_LIMIT = 63 * 1024 * 1024
LIGHT = pl.CostEstimate(flops=0, bytes_accessed=4096, transcendentals=0)


def split_bf16(x):
    high = x.astype(jnp.bfloat16)
    return high, (x - high.astype(jnp.float32)).astype(jnp.bfloat16)


def anywhere(count):
    return [pl.BlockSpec(memory_space=pl.ANY)] * count


def in_vmem(count):
    return [pl.BlockSpec(memory_space=pltpu.VMEM)] * count


def start(group):
    for copy in group:
        copy.start()


def wait(group):
    for copy in group:
        copy.wait()


def split_rows(where_ref, own, beside, first, held, sems, targets):
    size, width = targets[0].shape[0], own.shape[1]
    step = held.shape[2]
    places = (where_ref[1], 1 - where_ref[1])
    groups = [
        [
            pltpu.make_async_copy(source.at[pl.ds(first + row, step)], held.at[i, j], sems.at[i, j])
            for j, source in enumerate((own, beside))
        ]
        for i, row in enumerate(range(0, size, step))
    ]
    for copies in groups:
        start(copies)
    for i, copies in enumerate(groups):
        wait(copies)
        for j, place in enumerate(places):
            store_columns(targets, place, slice(i * step, (i + 1) * step), held[i, j])


def store_columns(targets, place, rows, values):
    width = values.shape[1]
    at = pl.ds(pl.multiple_of(place * width, width), width)
    for ref, value in zip(targets, split_bf16(values)):
        ref[rows, at] = value


def split_scratch(size, width):
    step = min(FACTOR_BLOCK, size)
    return [pltpu.VMEM((size // step, 2, step, width), jnp.float32), pltpu.SemaphoreType.DMA((size // step, 2))]


def below_kernel(tokens, where_ref, order_ref, own, beside, *refs):
    gathered, refs = refs[:4], refs[4 + tokens :]
    *targets, held, sems, parts, part_sems = refs
    size = targets[0].shape[0]

    @pl.when(where_ref[0] == 0)
    def _():
        split_rows(where_ref, own, beside, size, held, sems, targets)

    @pl.when(where_ref[0] != 0)
    def _():
        count, step = gathered[0].shape[:2]
        copies = [pltpu.make_async_copy(ref, parts.at[i], part_sems.at[i]) for i, ref in enumerate(gathered)]
        start(copies)
        for i, copy in enumerate(copies):
            copy.wait()
            place = where_ref[1] if i < 2 else 1 - where_ref[1]
            for j in range(count):
                rows = pl.ds(pl.multiple_of(order_ref[i % 2 * count + j] * step, step), step)
                store_columns(targets, place, rows, parts[i, j])


def split_below(where, order, own, beside, gathered, after):
    hours, width = own.shape
    half = hours // 2
    return pl.pallas_call(
        functools.partial(below_kernel, len(after)),
        in_specs=[pl.BlockSpec(memory_space=pltpu.SMEM)] * 2 + anywhere(6 + len(after)),
        out_specs=in_vmem(2),
        out_shape=[jax.ShapeDtypeStruct((half, 2 * width), jnp.bfloat16)] * 2,
        scratch_shapes=split_scratch(half, width)
        + [pltpu.VMEM((4, *gathered[0].shape), jnp.float32), pltpu.SemaphoreType.DMA((4,))],
        compiler_params=pltpu.CompilerParams(vmem_limit_bytes=VMEM_LIMIT),
        cost_estimate=LIGHT,
        name="split_below",
    )(where, order, own, beside, *gathered, *after)


def filter_kernel(first_col, cols, space_count, where_ref, left, centre, right, kappa_left, kappa, kappa_right, *refs):
    mine_ref, other_ref, wide, once, scale = refs[-5:]
    rows, width, lanes = centre.shape
    around = width + 2 * EDGE
    core, space = where_ref[1], where_ref[2]
    zero = jnp.zeros((around, lanes), jnp.float32)
    for ref in (wide, once):
        ref[0] = zero
        ref[rows + 1] = zero
    wide[1 : rows + 1, EDGE - left.shape[1] : EDGE, :] = left[...]
    wide[1 : rows + 1, EDGE : EDGE + width, :] = centre[...]
    wide[1 : rows + 1, EDGE + width : EDGE + width + right.shape[1], :] = right[...]

    @pl.when(pl.program_id(0) == 0)
    def _():
        weights = jnp.concatenate([kappa_left[...].T[-EDGE:], kappa[...].T, kappa_right[...].T[:EDGE]], axis=0) + 4.0
        weights = weights[first_col : first_col + around]
        for row in range(rows):
            scale[row] = jnp.broadcast_to(weights[:, row : row + 1], scale.shape[1:])

    strip = scale.shape[2]
    column = space * cols + first_col - EDGE + lax.broadcasted_iota(jnp.int32, (around, strip), 0)
    inside = (column >= 0) & (column < space_count * cols)

    def operate(source, row, at):
        x = source[row + 1, :, at]
        beside = source[row, :, at] + source[row + 2, :, at] + pltpu.roll(x, 1, 0) + pltpu.roll(x, around - 1, 0)
        return scale[row] * x - beside

    for place in range(lanes // strip):
        at = slice(place * strip, (place + 1) * strip)

        def first(row, carry):
            value = operate(wide, row, at)
            if first_col == 0 or first_col + width == cols:
                value = jnp.where(inside, value, 0.0)
            once[row + 1, :, at] = value
            return carry

        def second(row, carry):
            mine_ref[row, :, at] = operate(once, row + core * (rows // 2), at)[EDGE : EDGE + width]
            other_ref[row, :, at] = operate(once, row + (1 - core) * (rows // 2), at)[EDGE : EDGE + width]
            return carry

        lax.fori_loop(0, rows, first, 0, unroll=12)
        lax.fori_loop(0, rows // 2, second, 0, unroll=6)


def filtered(where, latent, halos, kappa_sq, start, width, space_count, after):
    rows, cols, hours = latent.shape
    lanes = min(2 * LANES, hours)
    last = start + width

    def spec(columns, index):
        return pl.BlockSpec((rows, columns, lanes), lambda i, w: (0, index, i))

    low, high = halos
    left = (low, spec(low.shape[1], 0)) if start == 0 else (latent, spec(EDGE, start // EDGE - 1))
    centre = (latent, spec(width, start // width))
    right = (high, spec(high.shape[1], 0)) if last == cols else (latent, spec(EDGE, last // EDGE))
    fields, specs = zip(left, centre, right)
    kappa_specs = [
        pl.BlockSpec((rows, cols), lambda i, w, step=step: (0, jnp.clip(w[2] + step, 0, space_count - 1)))
        for step in (-1, 0, 1)
    ]
    half = rows // 2
    return pl.pallas_call(
        functools.partial(filter_kernel, start, cols, space_count),
        grid_spec=pltpu.PrefetchScalarGridSpec(
            num_scalar_prefetch=1,
            grid=(hours // lanes,),
            in_specs=[*specs, *kappa_specs] + anywhere(len(after)),
            out_specs=[pl.BlockSpec((half, width, lanes), lambda i, w: (0, 0, i))] * 2,
            scratch_shapes=[pltpu.VMEM((rows + 2, width + 2 * EDGE, lanes), jnp.float32)] * 2
            + [pltpu.VMEM((rows, width + 2 * EDGE, min(LANES, hours)), jnp.float32)],
        ),
        out_shape=[jax.ShapeDtypeStruct((half, width, hours), jnp.float32)] * 2,
        compiler_params=pltpu.CompilerParams(vmem_limit_bytes=VMEM_LIMIT),
        cost_estimate=LIGHT,
        name="filter",
    )(where, *fields, *[kappa_sq] * 3, *after)


def multiply(parts, weights, contract):
    (x_high, x_low), (w_high, w_low) = parts, weights
    dot = functools.partial(
        lax.dot_general,
        dimension_numbers=(((1,), (contract,)), ((), ())),
        preferred_element_type=jnp.float32,
    )
    return dot(x_high, w_high) + (dot(x_low, w_high) + dot(x_high, w_low))


def cut(refs, rows, columns):
    return tuple(ref[rows, columns] for ref in refs)


def blocks(size):
    step = min(FACTOR_BLOCK, size // 2)
    return [slice(i, i + step) for i in range(0, size, step)]


def place_series(source, parts):
    hours = source.shape[2]
    for place in range(2):
        for ref, value in zip(parts, split_bf16(source[place])):
            ref[:, place * hours : (place + 1) * hours] = value


def hours_of(at, size):
    place = at.start // (size // 2)
    return place, slice(at.start - place * size // 2, at.stop - place * size // 2)


def load(weights, buffer, sems):
    return [pltpu.make_async_copy(ref, buffer.at[part], sems.at[part]) for part, ref in enumerate(weights)]


def weight_scratch(size):
    return [pltpu.VMEM((2, size, size), jnp.bfloat16)], [pltpu.SemaphoreType.DMA((2,))]


def begin_kernel(tokens, first, where_ref, mine, across, *refs):
    refs = refs[tokens:]
    if first:
        own, beside, sent, sums, *parts = refs[:6]
        fields, series, middle, held, diagonal, sems, part_sems, rows_held, rows_sems = refs[6:]
    else:
        weights, sent, sums = refs[:2], *refs[2:4]
        fields, series, middle, held, diagonal, sems, weight_sems = refs[4:]
    size = held.shape[1]
    core = where_ref[1]
    everything = slice(None)
    series, middle = [series.at[i] for i in range(2)], [middle.at[i] for i in range(2)]
    lower = where_ref[0] == 0
    upper = jnp.logical_not(lower)
    inputs = [
        pltpu.make_async_copy(mine, fields.at[core], sems.at[0]),
        pltpu.make_async_copy(across, fields.at[1 - core], sems.at[1]),
    ]
    hours = size // 2
    forward = [
        pltpu.make_async_copy(fields.at[i], sent.at[:, i * hours : (i + 1) * hours], sems.at[2 + i]) for i in range(2)
    ]
    start(inputs)
    if first:
        stores = [pltpu.make_async_copy(diagonal.at[i], part, part_sems.at[i]) for i, part in enumerate(parts)]
        diagonal = [diagonal.at[i] for i in range(2)]
        split_rows(where_ref, own, beside, where_ref[0] * size, rows_held, rows_sems, diagonal)
        start(stores)
    else:
        loads = load(weights, diagonal, weight_sems)
        diagonal = [diagonal.at[i] for i in range(2)]
        start(loads)
    wait(inputs)

    @pl.when(upper)
    def _():
        start(forward)

    place_series(fields, series)
    if not first:
        wait(loads)
    for at in blocks(size):
        rows = slice(at.start, size)
        held[:, at] = multiply(cut(series, everything, rows), cut(diagonal, rows, at), 0)

    @pl.when(lower)
    def _():
        output = pltpu.make_async_copy(held, sent, sems.at[4])
        output.start()
        output.wait()

    @pl.when(upper)
    def _():
        for ref, part in zip(middle, split_bf16(held[...])):
            ref[...] = part
        for at in blocks(size):
            columns = slice(0, at.stop)
            held[:, at] = multiply(cut(middle, everything, columns), cut(diagonal, at, columns), 1)
        output = pltpu.make_async_copy(held, sums, sems.at[4])
        output.start()
        wait(forward)
        output.wait()

    if first:
        wait(stores)


def begin(where, mine, across, diagonal, after, columns=None):
    cells, hours = mine.shape
    size = 2 * hours
    operands = [mine, across, *after, *(columns or diagonal)]
    first = columns is not None
    outs = [jax.ShapeDtypeStruct((cells, size), jnp.float32)] * 2
    buffers, sems = weight_scratch(size)
    scratch = [
        pltpu.VMEM((2, cells, hours), jnp.float32),
        pltpu.VMEM((2, cells, size), jnp.bfloat16),
        pltpu.VMEM((2, cells, size), jnp.bfloat16),
        pltpu.VMEM((cells, size), jnp.float32),
        *buffers,
        pltpu.SemaphoreType.DMA((5,)),
        *sems,
    ]
    if first:
        outs = outs + [jax.ShapeDtypeStruct((size, size), jnp.bfloat16)] * 2
        scratch = scratch + split_scratch(size, hours)
    return pl.pallas_call(
        functools.partial(begin_kernel, len(after), first),
        in_specs=[pl.BlockSpec(memory_space=pltpu.SMEM)] + anywhere(len(operands)),
        out_specs=anywhere(len(outs)),
        out_shape=outs,
        scratch_shapes=scratch,
        compiler_params=pltpu.CompilerParams(vmem_limit_bytes=VMEM_LIMIT),
        cost_estimate=LIGHT,
        name="begin",
    )(where, *operands)


def send_hours(core, place, results, targets, sem):
    for target, chosen in zip(targets, (core == place, core != place)):

        @pl.when(chosen)
        def _():
            pltpu.make_async_copy(results.at[place], target, sem).start()


def wait_hours(core, results, targets, sems):
    for place in range(2):
        for target, chosen in zip(targets, (core == place, core != place)):

            @pl.when(chosen)
            def _():
                pltpu.make_async_copy(results.at[place], target, sems[place]).wait()


def end_kernel(tokens, where_ref, sent, sums, arrived, *refs):
    refs = refs[tokens:]
    diagonal_parts, below_parts, targets, refs = refs[:2], refs[2:4], refs[4:6], refs[6:]
    factors, terms, held, series, middle, results, diagonal, below, sems, diagonal_sems, below_sems = refs
    size = factors.shape[1]
    core = where_ref[1]
    everything = slice(None)
    series, middle = [series.at[i] for i in range(2)], [middle.at[i] for i in range(2)]
    lower = where_ref[0] == 0
    upper = jnp.logical_not(lower)

    def inputs(field, term):
        return [
            pltpu.make_async_copy(field, factors, sems.at[0]),
            pltpu.make_async_copy(term, terms, sems.at[1]),
        ]

    before = pltpu.make_async_copy(sums, held, sems.at[2])
    diagonal_loads = load(diagonal_parts, diagonal, diagonal_sems)
    halves = [slice(0, size // 2), slice(size // 2, size)]
    below_loads = [
        [
            pltpu.make_async_copy(ref.at[rows, :], below.at[part, rows, :], below_sems.at[part, i])
            for part, ref in enumerate(below_parts)
        ]
        for i, rows in enumerate(halves)
    ]
    diagonal, below = ([x.at[i] for i in range(2)] for x in (diagonal, below))

    @pl.when(lower)
    def _():
        start(inputs(arrived, sent))

    @pl.when(upper)
    def _():
        start(inputs(sent, arrived))

    for copies in below_loads:
        start(copies)

    @pl.when(lower)
    def _():
        start(diagonal_loads)

    @pl.when(upper)
    def _():
        before.start()

    @pl.when(lower)
    def _():
        wait(inputs(arrived, sent))

    @pl.when(upper)
    def _():
        wait(inputs(sent, arrived))

    for ref, part in zip(series, split_bf16(factors[...])):
        ref[...] = part
    for rows, copies in zip(halves, below_loads):
        wait(copies)
        for at in blocks(size):
            value = terms[:, at] + multiply(cut(series, everything, rows), cut(below, rows, at), 0)
            if rows.stop < size:
                terms[:, at] = value
            else:
                for ref, part in zip(middle, split_bf16(value)):
                    ref[:, at] = part

    @pl.when(lower)
    def _():
        wait(diagonal_loads)

    @pl.when(upper)
    def _():
        before.wait()

    for at in blocks(size):
        columns = slice(0, at.stop)
        place, piece = hours_of(at, size)

        @pl.when(lower)
        def _():
            results[place, :, piece] = multiply(cut(middle, everything, columns), cut(diagonal, at, columns), 1)

        @pl.when(upper)
        def _():
            value = multiply(cut(middle, everything, everything), cut(below, at, everything), 1)
            results[place, :, piece] = held[:, at] + value

        if at.stop == (place + 1) * size // 2:
            send_hours(core, place, results, targets, sems.at[3 + place])
    wait_hours(core, results, targets, [sems.at[3], sems.at[4]])


def end(where, sent, sums, arrived, diagonal, below, after):
    cells, size = sent.shape
    hours = size // 2
    operands = [sent, sums, arrived, *after]
    return pl.pallas_call(
        functools.partial(end_kernel, len(after)),
        in_specs=[pl.BlockSpec(memory_space=pltpu.SMEM)] + anywhere(len(operands) + 4),
        out_specs=anywhere(2),
        out_shape=[jax.ShapeDtypeStruct((cells, hours), jnp.float32)] * 2,
        scratch_shapes=[pltpu.VMEM((cells, size), jnp.float32)] * 3
        + [pltpu.VMEM((2, cells, size), jnp.bfloat16)] * 2
        + [pltpu.VMEM((2, cells, hours), jnp.float32)]
        + weight_scratch(size)[0] * 2
        + [pltpu.SemaphoreType.DMA((5,)), pltpu.SemaphoreType.DMA((2,)), pltpu.SemaphoreType.DMA((2, 2))],
        compiler_params=pltpu.CompilerParams(vmem_limit_bytes=VMEM_LIMIT),
        cost_estimate=LIGHT,
        name="end",
    )(where, *operands, *diagonal, *below)


def join_kernel(count, *refs):
    out, held, sems = refs[-3:]
    first = 0
    group = []
    for i, ref in enumerate(refs[:count]):
        group.append(pltpu.make_async_copy(ref, held.at[pl.ds(first, ref.shape[0])], sems.at[i]))
        first += ref.shape[0]
    start(group)
    wait(group)
    output = pltpu.make_async_copy(held, out, sems.at[count])
    output.start()
    output.wait()


def join(pieces, after):
    shape = (sum(x.shape[0] for x in pieces), *pieces[0].shape[1:])
    return pl.pallas_call(
        functools.partial(join_kernel, len(pieces)),
        in_specs=anywhere(len(pieces) + len(after)),
        out_specs=pl.BlockSpec(memory_space=pl.ANY),
        out_shape=jax.ShapeDtypeStruct(shape, pieces[0].dtype),
        scratch_shapes=[pltpu.VMEM(shape, pieces[0].dtype), pltpu.SemaphoreType.DMA((len(pieces) + 1,))],
        compiler_params=pltpu.CompilerParams(vmem_limit_bytes=VMEM_LIMIT),
        cost_estimate=LIGHT,
        name="join",
    )(*pieces, *after)


def finish_kernel(turns, where_ref, step_ref, own, beside, latent_ref, events_ref, base_ref, draw_ref, *refs):
    gradient_ref, proposal_ref = refs[-2:]
    latent = latent_ref[...]
    spread = jnp.sqrt(jnp.full((1, 1, latent.shape[2]), 2.0 * step_ref[0]))
    data = events_ref[...].astype(jnp.float32) - jnp.exp(base_ref[...] + latent)
    for i, turn in enumerate(turns):
        prior = (own, beside)[turn]

        @pl.when(pl.program_id(0) == i)
        def _():
            slope = data - prior[...]
            gradient_ref[...] = slope
            proposal_ref[...] = latent + step_ref[0] * slope + spread * draw_ref[...]


def finish(where, steps, priors, fields, start, width, outs, after, turns):
    rows, cols, hours = fields[0].shape
    half = rows // 2
    shape = (half, width, hours)
    held = [prior.reshape(shape) for prior in priors]
    held_spec = pl.BlockSpec(shape, lambda i, w, s: (0, 0, 0))
    field_spec = pl.BlockSpec(shape, lambda i, w, s: ((w[1] + i + turns[0]) % 2, start // width, 0))
    out = jax.ShapeDtypeStruct((rows, cols, hours), jnp.float32)
    return pl.pallas_call(
        functools.partial(finish_kernel, turns),
        grid_spec=pltpu.PrefetchScalarGridSpec(
            num_scalar_prefetch=2,
            grid=(len(turns),),
            in_specs=[held_spec] * 2 + [field_spec] * 4 + anywhere(len(outs) + len(after)),
            out_specs=[field_spec] * 2,
        ),
        out_shape=[out, out],
        input_output_aliases={8 + i: i for i in range(len(outs))},
        compiler_params=pltpu.CompilerParams(vmem_limit_bytes=VMEM_LIMIT),
        cost_estimate=LIGHT,
        name="finish",
    )(where, steps, *held, *fields, *outs, *after)


def local(latent, events, log_base, innovation, kappa_sq, chol_factor, step_size):
    rows, cols, hours = latent.shape
    place = lax.axis_index("tm")
    upper, core = place // 2, place % 2
    space = lax.axis_index("space")
    space_count = lax.axis_size("space")
    where = jnp.stack([upper, core, space]).astype(jnp.int32)

    def beside(x):
        return lax.ppermute(x, "tm", [(0, 1), (1, 0), (2, 3), (3, 2)])

    def exchange(x):
        return lax.ppermute(x, "tm", [(0, 2), (1, 3), (2, 0), (3, 1)])

    across_core = beside(chol_factor)
    forward = [(i, i + 1) for i in range(space_count - 1)]
    backward = [(i + 1, i) for i in range(space_count - 1)]
    halos = (
        lax.ppermute(latent[:, cols - 2 :], "space", forward),
        lax.ppermute(latent[:, :2], "space", backward),
    )
    fields = (latent, events, log_base, innovation)
    mine, others, sent, sums, arrived, totals = ({} for _ in range(6))

    share = 2 * hours // space_count
    slab = lax.dynamic_slice(chol_factor, (2 * hours + space * share, jnp.int32(0)), (share, hours))
    held = lax.ppermute(slab, "tm", [(0, 2), (1, 3)])[None]
    order = [0]

    def double(x):
        bit = space_count // 2 // len(order)
        order.extend([i ^ bit for i in order])
        return lax.ppermute(x, "space", [(i, i ^ bit) for i in range(space_count)])

    received = double(held)
    transfers = {"slab": [held], "halo": [*halos]}
    token, outs, diagonal = [], [], []
    for name in ORDER:
        kind, k = name[0], int(name[1:] or 0)
        after = token + [x for pin in PINS.get(name, ()) for x in transfers[pin]]
        if kind == "F":
            made = filtered(where, latent, halos, kappa_sq, *CHUNKS[k], space_count, after)
            mine[k], away = (x.reshape(-1, hours) for x in made)
            others[k] = beside(away)
            token = [mine[k]]
        elif kind == "B":
            columns = None if diagonal else (chol_factor, across_core)
            sent[k], sums[k], *parts = begin(where, mine[k], others[k], diagonal, after, columns)
            diagonal = diagonal or parts
            arrived[k] = exchange(sent[k])
            transfers["Y" + name[1:]] = [arrived[k]]
            token = [sent[k]]
        elif kind == "J" and k < 3:
            held = join([held, received], after)
            received = double(held)
            token = [held]
        elif kind == "J":
            received = join([received], after)
            token = [received]
        elif kind == "S":
            gathered = [held, received, beside(held), beside(received)]
            order = space.astype(jnp.int32) ^ jnp.array(order, jnp.int32)
            below = split_below(where, order, chol_factor, across_core, gathered, after)
            token = [below[0]]
        elif kind == "E":
            own, across = end(where, sent[k], sums[k], arrived[k], diagonal, below, after)
            totals[k] = own, beside(across)
            token = [own]
        else:
            own, across = totals[k]
            turns = {"f": (0, 1), "g": (0,), "h": (1,)}[kind]
            priors = (own, own) if kind == "g" else (own, across)
            after = [x for x in after if not any(x is y for y in outs)]
            outs = finish(where, step_size, priors, fields, *CHUNKS[k], outs, after, turns)
            token = [outs[0]]
    return outs


def plain(latent, events, log_base, innovation, kappa_sq, chol_factor, step_size):
    rows, cols, hours = latent.shape
    space = lax.axis_index("space")
    count = lax.axis_size("space")
    forward = [(i, i + 1) for i in range(count - 1)]
    backward = [(i + 1, i) for i in range(count - 1)]
    kappa = lax.dynamic_slice(kappa_sq, (jnp.int32(0), space * cols), (rows, cols))

    def operate(field):
        low = lax.ppermute(field[:, -1:], "space", forward)
        high = lax.ppermute(field[:, :1], "space", backward)
        row_padded = jnp.pad(field, ((1, 1), (0, 0), (0, 0)))
        wide = jnp.concatenate([low, field, high], axis=1)
        beside = row_padded[2:] + row_padded[:-2] + wide[:, 2:] + wide[:, :-2]
        return (kappa[:, :, None] + 4.0) * field - beside

    dot = functools.partial(lax.dot_general, precision=lax.Precision.HIGHEST, preferred_element_type=jnp.float32)
    series = operate(operate(latent)).reshape(rows * cols, hours)
    projected = dot(lax.all_gather(series, "tm", axis=1, tiled=True), chol_factor, (((1,), (0,)), ((), ())))
    sums = dot(chol_factor, projected, (((1,), (1,)), ((), ())))
    by_hour = lax.psum_scatter(sums, "tm", scatter_dimension=0, tiled=True)
    prior = by_hour.T.reshape(rows, cols, hours)
    gradient = events.astype(jnp.float32) - jnp.exp(log_base + latent) - prior
    proposal = latent + step_size[0] * gradient + jnp.sqrt(2.0 * step_size[0]) * innovation
    return gradient, proposal


def solution(mesh):
    in_specs = (
        P(None, "space", "tm"),
        P(None, "space", "tm"),
        P(None, "space", "tm"),
        P(None, "space", "tm"),
        P(),
        P(None, "tm"),
        P(),
    )
    out_specs = (P(None, "space", "tm"), P(None, "space", "tm"))
    body = local if mesh.shape["tm"] == 4 and mesh.shape["space"] == 8 else plain
    return jax.shard_map(body, mesh=mesh, in_specs=in_specs, out_specs=out_specs, check_vma=False)
```
